256 devices in a mesh: row: 8 (over z), col: 32 (over y, x, core).
Axes of the slice: x: 4, y: 4, z: 8, core: 2. Of those that a mesh axis runs over, the one named last changes fastest.
Arguments:
- precision_diag: float32 [256, 256, 256], P(('row', 'col')), may hold values from -0.1 to 4.6, as said below
- precision_pairs: float32 [256, 7, 256, 256], P(('row', 'col')), may hold values from -0.024 to 0.024
- pattern_cols: int32 [256, 7], P(('row', 'col')), may hold values from -1 to 255, as said below
- newton_diag: float32 [256, 256, 256], P(('row', 'col')), may hold values from -0.1 to 0.1, as said below
- newton_pairs: float32 [256, 7, 256, 256], P(('row', 'col')), may hold values from -0.006 to 0.006
- warm_start: float32 [256, 96, 256], P(('row', 'col')), may hold values from -15 to 15
- target_rows: int32 [96], replicated, may hold values from 0 to 65535, as said below
Outputs:
- inverse_panel: float32 [256, 96, 256], P(('row', 'col'))
- hessian_block: float32 [96, 96], P('row', 'col')
The draws below stay inside these ranges and needn't reach their ends.
Inputs may be any that keep to these rules, and one draw needn't show every extreme that they name: `pattern_cols`: each row lists its live entries first and -1 for the rest; it has 4 to 7 live entries, some row exactly 7 and some fewer. The live entries of block row I are distinct, differ from I, and lie in the group of 32 consecutive block rows that holds I (groups start at multiples of 32). `precision_diag`: each tile is symmetric, and X is positive definite. `newton_diag`: each tile is symmetric. `target_rows`: the 96 entries are distinct rows of X.
All inputs are finite; a program needn't handle non-finite values.
Results may differ from the reference program's by a relative error of at most 0.0003.
Values sent between devices are 32-bit elements; how exact they have to be, the bound alone decides.
A program may use at most 64 MiB of HBM per device.

```python
import math
import jax
import jax.numpy as jnp
from jax import lax

B = 256
PAIR_CAP = 7
C = 96
NB = 256
GROUP_BLOCK_ROWS = 32


def symmetric_part(entries, scale):
    return (entries + jnp.swapaxes(entries, 1, 2)) * (scale / math.sqrt(2.0))


def draw_precision_diag(key, part):
    first_key, second_key = jax.random.split(jax.random.fold_in(key, 101))
    entries = jnp.clip(jax.random.normal(first_key, (NB, B, B), jnp.float32), -6.0, 6.0)
    diagonal_entries = jnp.exp(jax.random.uniform(second_key, (NB, B), jnp.float32, math.log(1.5), math.log(4.5)))
    identity = jnp.eye(B, dtype=jnp.float32)
    return symmetric_part(entries, 0.08 / math.sqrt(B)) + identity[None, :, :] * diagonal_entries[:, :, None]


def draw_newton_diag(key, part):
    first_key = jax.random.fold_in(jax.random.fold_in(key, 202), 0)
    entries = jnp.clip(jax.random.normal(first_key, (NB, B, B), jnp.float32), -6.0, 6.0)
    return symmetric_part(entries, 0.016 / math.sqrt(B))


def draw_warm_start(key, part):
    first_key, second_key = jax.random.split(jax.random.fold_in(key, 303))
    growth = 0.5 * 3.0 ** (jnp.arange(NB, dtype=jnp.float32) / NB)
    entries = jnp.clip(jax.random.normal(first_key, (NB, C, B), jnp.float32), -5.0, 5.0)
    rough = jnp.exp(jax.random.uniform(second_key, (NB, C, B), jnp.float32, math.log(0.5), math.log(2.0)))
    return entries * rough * growth[:, None, None]


def draw_pattern_cols(key, part):
    first_key, second_key, third_key = jax.random.split(jax.random.fold_in(key, 404), 3)
    row_index = jnp.arange(NB, dtype=jnp.int32)
    slot_location = row_index % GROUP_BLOCK_ROWS
    counts = jax.random.randint(first_key, (NB,), 4, PAIR_CAP + 1)
    counts = jnp.where(slot_location == 0, PAIR_CAP, counts)
    counts = jnp.where(slot_location == 1, 4, counts)
    hub_slots = jax.random.randint(second_key, (NB // GROUP_BLOCK_ROWS,), 0, GROUP_BLOCK_ROWS)
    hub_row = hub_slots[row_index // GROUP_BLOCK_ROWS]
    candidate_items = jnp.arange(GROUP_BLOCK_ROWS, dtype=jnp.int32)
    rank_scores = jax.random.randint(third_key, (NB, GROUP_BLOCK_ROWS), 0, 1 << 20) * GROUP_BLOCK_ROWS + candidate_items[None, :]
    rank_scores = jnp.where(candidate_items[None, :] == hub_row[:, None], rank_scores + (1 << 29), rank_scores)
    final_reward = (candidate_items[None, :] == GROUP_BLOCK_ROWS - 1) & (slot_location[:, None] == 0)
    rank_scores = jnp.where(final_reward, rank_scores + (1 << 28), rank_scores)
    rank_scores = jnp.where(candidate_items[None, :] == slot_location[:, None], -1, rank_scores)
    ranking = jnp.argsort(-rank_scores, axis=1, stable=True)[:, :PAIR_CAP]
    columns = (row_index - slot_location)[:, None] + ranking
    live_mask = jnp.arange(PAIR_CAP)[None, :] < counts[:, None]
    return jnp.where(live_mask, columns, -1).astype(jnp.int32)


def draw_target_rows(key, part):
    first_key, second_key = jax.random.split(jax.random.fold_in(key, 505))
    inner = jax.random.permutation(first_key, NB * B - 2)[:C - 2].astype(jnp.int32) + 1
    ends = jnp.array([0, NB * B - 1], dtype=jnp.int32)
    chosen = jnp.concatenate([ends, inner])
    return jax.random.permutation(second_key, chosen).astype(jnp.int32)


def levels(own_key, extent, pieces, low, largest):
    def one(dim, parts):
        draws = jax.random.uniform(jax.random.fold_in(jax.random.fold_in(own_key, 6), dim), (parts,), jnp.float32, low / len(pieces), largest / len(pieces))
        return jnp.repeat(jnp.exp(draws), extent[dim] // parts).reshape((-1,) + (1,) * (len(extent) - dim - 1))

    level = one(*pieces[0])
    for cut in pieces[1:]:
        level = level * one(*cut)
    return level


def normal_values(key, shape, width, most, cuts=(), kind=jnp.bfloat16):
    values = jax.random.normal(key, shape, jnp.float32) * width
    if len(cuts) > 0:
        values = levels(key, shape, cuts, -0.22, 0.18) * values
    return jnp.clip(values, min=-most, max=most).astype(kind)


def setup_inputs(seed: int = 0) -> dict:
    streams_of = jax.random.split(jax.random.key(seed), 8)
    precision_diag = draw_precision_diag(jax.random.fold_in(streams_of[7], 71), 0)
    precision_pairs = normal_values(streams_of[1], (NB, PAIR_CAP, B, B), (0.064 / B ** 0.5), 0.024, ((0, 256),), jnp.float32)
    pattern_cols = draw_pattern_cols(jax.random.fold_in(streams_of[7], 71), 0)
    newton_diag = draw_newton_diag(jax.random.fold_in(streams_of[7], 71), 0)
    newton_pairs = normal_values(streams_of[4], (NB, PAIR_CAP, B, B), (0.016 / B ** 0.5), 0.006, ((0, 256),), jnp.float32)
    warm_start = draw_warm_start(jax.random.fold_in(streams_of[7], 71), 0)
    target_rows = draw_target_rows(jax.random.fold_in(streams_of[7], 71), 0)
    return {"precision_diag": precision_diag, "precision_pairs": precision_pairs, "pattern_cols": pattern_cols, "newton_diag": newton_diag, "newton_pairs": newton_pairs, "warm_start": warm_start, "target_rows": target_rows}


HIGHEST = lax.Precision.HIGHEST


def apply_blocks(blocks, diag_tiles, pair_tiles, pattern_cols):
    live_mask = pattern_cols >= 0
    safe_cols = jnp.where(live_mask, pattern_cols, 0).astype(jnp.int32)
    weights = live_mask.astype(jnp.float32)[:, :, None, None]
    blocks = blocks.astype(jnp.float32)
    diag_tiles = diag_tiles.astype(jnp.float32)
    pair_tiles = pair_tiles.astype(jnp.float32)
    picked = blocks[safe_cols] * weights
    own_rows = jnp.einsum("icb,iab->ica", blocks, diag_tiles, precision=HIGHEST)
    own_rows = own_rows + jnp.einsum("ikcb,ikab->ica", picked, pair_tiles, precision=HIGHEST)
    moved_terms = jnp.einsum("icb,ikba->ikca", blocks, pair_tiles, precision=HIGHEST) * weights
    spread = jnp.zeros_like(blocks).at[safe_cols.reshape(-1)].add(moved_terms.reshape((-1,) + blocks.shape[1:]))
    return own_rows + spread


def column_dots(first, second):
    return jnp.sum(first * second, axis=(0, 2))


def reference(precision_diag, precision_pairs, pattern_cols, newton_diag, newton_pairs, warm_start, target_rows):
    global_rows = jnp.arange(NB * B, dtype=jnp.int32).reshape(NB, 1, B)
    unit_columns = (global_rows == target_rows[None, :, None]).astype(jnp.float32)
    solution = warm_start
    residual = unit_columns - apply_blocks(solution, precision_diag, precision_pairs, pattern_cols)
    norm_now = column_dots(residual, residual)
    direction = residual
    for iteration in range(2):
        images = apply_blocks(direction, precision_diag, precision_pairs, pattern_cols)
        step_size = norm_now / column_dots(direction, images)
        solution = solution + step_size[None, :, None] * direction
        if iteration == 0:
            residual = residual - step_size[None, :, None] * images
            norm_next = column_dots(residual, residual)
            direction = residual + (norm_next / norm_now)[None, :, None] * direction
            norm_now = norm_next
    newton_image = apply_blocks(solution, newton_diag, newton_pairs, pattern_cols)
    hessian = jnp.einsum("icb,idb->cd", solution, newton_image, precision=HIGHEST)
    return solution, hessian
```

```python
import jax
import jax.numpy as jnp
from jax import lax
from jax.experimental import pallas as pl
from jax.experimental.pallas import tpu as pltpu
from jax.sharding import PartitionSpec as P

HIGHEST = lax.Precision.HIGHEST
MESH = pl.DeviceIdType.MESH
F32, BF16, I32 = jnp.float32, jnp.bfloat16, jnp.int32
C, B, K = 96, 256, 7
HALF = C // 2
PLANE, DEPTH, SIDE = 32, 8, 4
NT = (((1,), (1,)), ((), ()))
NN = (((1,), (0,)), ((), ()))
OFFS = (0, -1, 1, 2)
ZERO_BLOCK = PLANE
ZERO_TERM = K
N_AG, N_RS = 35, 20


def split(v):
    high = v.astype(BF16)
    return high, (v - high.astype(F32)).astype(BF16)


def product(v, high_tile, low_tile, dims):
    high, low = split(v)
    both = lax.dot_general(
        jnp.concatenate([high, low], axis=0), high_tile, dims, preferred_element_type=F32
    )
    rest = lax.dot_general(high, low_tile, dims, preferred_element_type=F32)
    return both[: v.shape[0]] + both[v.shape[0] :] + rest


def sums_to_rows(pairs):
    lane = lax.broadcasted_iota(I32, (C, 128), 1)
    wide = jnp.zeros((C, 128), F32)
    for i, (first, second) in enumerate(pairs):
        wide = jnp.where(lane == i, jnp.sum(first * second, axis=1, keepdims=True), wide)
    wide = jnp.concatenate([wide, jnp.zeros((128 - C, 128), F32)], axis=0)
    return jnp.transpose(wide)[0:8]


def rows_to_columns(tile):
    wide = jnp.concatenate([tile, jnp.zeros((120, 128), F32)], axis=0)
    return jnp.transpose(wide)[0:C]


class Place:
    def __init__(self):
        self.row = lax.axis_index("row")
        self.col = lax.axis_index("col")
        col = self.col
        self.core = lax.rem(col, 2)
        x, y = lax.rem(col // 2, SIDE), col // (2 * SIDE)
        core = self.core
        self.a, self.b = x + core * (y - x), y + core * (x - y)
        self.sa, self.sb = 2 + 6 * core, 8 - 6 * core
        self.sibling = col + 1 - 2 * core

    def block(self, da, db):
        return (
            lax.rem(self.a + da + SIDE, SIDE) * self.sa
            + lax.rem(self.b + db + SIDE, SIDE) * self.sb
            + self.core
        )

    def sibling_block(self, da, db):
        return (
            lax.rem(self.b + da + SIDE, SIDE) * self.sb
            + lax.rem(self.a + db + SIDE, SIDE) * self.sa
            + (1 - self.core)
        )


class Gather:
    def __init__(self, place, panel, send_sems, recv_sems):
        self.p, self.panel, self.ss, self.rs = place, panel, send_sems, recv_sems
        self.sent = []

    def copy(self, slot, device, index, half=None):
        part = self.panel.at[slot] if half is None else self.panel.at[slot, pl.ds(half * HALF, HALF)]
        return pltpu.make_async_remote_copy(
            part, part, self.ss.at[index], self.rs.at[index], device_id=(self.p.row, device), device_id_type=MESH
        )

    def send(self, *args):
        copy = self.copy(*args)
        copy.start()
        self.sent.append(copy)

    def wait(self, slot, index, half=None):
        self.copy(slot, self.p.sibling, index, half).wait_recv()

    def along_b(self, i):
        p = self.p
        slot = p.block(OFFS[i], 0)
        self.send(slot, p.block(0, 1), 3 + 2 * i)
        self.send(slot, p.block(0, -1), 4 + 2 * i)
        self.send(slot, p.sibling, 19 + 4 * i)

    def begin(self):
        p = self.p
        for n, da in enumerate((1, -1, 2)):
            self.send(p.col, p.block(da, 0), n)
        self.along_b(0)

    def first(self):
        for i in (1, 2, 3):
            self.wait(self.p.block(OFFS[i], 0), i - 1)
            self.along_b(i)

    def second(self, i):
        p = self.p
        for side, db in ((0, -1), (1, 1)):
            slot = p.block(OFFS[i], db)
            self.wait(slot, 3 + 2 * i + side)
            self.send(slot, p.block(0, -db), 11 + 2 * i + side, side)
            self.send(slot, p.sibling, 20 + 4 * i + side)

    def third(self, i):
        slot = self.p.block(OFFS[i], 2)
        for side in (0, 1):
            self.wait(slot, 11 + 2 * i + side, side)
        self.send(slot, self.p.sibling, 22 + 4 * i)

    def end(self):
        for i in range(SIDE):
            for j in range(SIDE):
                self.wait(self.p.sibling_block(OFFS[i], OFFS[j]), 19 + 4 * i + j)

    def drain(self):
        for copy in self.sent:
            copy.wait_send()


class Scatter:
    def __init__(self, place, term, other, fwd_out, fwd_in, main_out, main_in, last_out, last_in, ss, rs, own, theirs):
        self.p, self.term, self.other = place, term, other
        self.fwd_out, self.fwd_in = fwd_out, fwd_in
        self.main_out, self.main_in = main_out, main_in
        self.last_out, self.last_in = last_out, last_in
        self.ss, self.rs, self.own, self.theirs = ss, rs, own, theirs
        self.sent = []

    def copy(self, src, dst, device, index):
        return pltpu.make_async_remote_copy(
            src, dst, self.ss.at[index], self.rs.at[index], device_id=(self.p.row, device), device_id_type=MESH
        )

    def send(self, *args):
        copy = self.copy(*args)
        copy.start()
        self.sent.append(copy)

    def arrived(self, ref, index):
        self.copy(ref, ref, self.p.sibling, index).wait_recv()

    def begin(self, k):
        self.send(self.term.at[k], self.other.at[k], self.p.sibling, k)

    def terms(self):
        for k in range(K):
            self.arrived(self.other.at[k], k)

    def share(self, da, db):
        block = self.p.block(da, db)
        mine, others = ZERO_TERM, ZERO_TERM
        for k in range(K):
            mine = jnp.where(self.own(k) == block, k, mine)
            others = jnp.where(self.theirs(k) == block, k, others)
        return self.term[mine] + self.other[others]

    def forward(self):
        p = self.p
        for side, da in ((0, 1), (1, -1)):
            for j in (0, 1):
                self.fwd_out[side, j] = self.share(2, OFFS[2 * side + j])
            self.send(self.fwd_out.at[side], self.fwd_in.at[side], p.block(da, 0), K + side)

    def main(self, side, j, extra=None):
        da = 1 - 2 * side
        value = self.share(da, OFFS[j])
        if extra is not None:
            value = value + self.fwd_in[side, extra]
        self.main_out[side, j] = value
        self.send(self.main_out.at[side, j], self.main_in.at[side, j], self.p.block(da, 0), K + 2 + SIDE * side + j)

    def main_free(self):
        for j in (0, 1):
            self.main(0, 2 + j)
            self.main(1, j)

    def main_rest(self):
        for side in (0, 1):
            self.arrived(self.fwd_in.at[side], K + side)
            for j in (0, 1):
                self.main(side, 2 * side + j, j)

    def last(self):
        for j in (2, 1, 3, 0):
            for side in (0, 1):
                self.arrived(self.main_in.at[side, j], K + 2 + SIDE * side + j)
            self.last_out[j] = self.share(0, OFFS[j]) + self.main_in[0, j] + self.main_in[1, j]
            if j:
                self.send(self.last_out.at[j], self.last_in.at[j - 1], self.p.block(0, OFFS[j]), 16 + j)

    def result(self):
        for j in (1, 2, 3):
            self.arrived(self.last_in.at[j - 1], 16 + j)
        return self.last_out[0] + self.last_in[0] + self.last_in[1] + self.last_in[2]

    def drain(self):
        for copy in self.sent:
            copy.wait_send()


class Total:
    def __init__(self, place, source, mid, plane_in, depth_in, sems):
        self.p, self.source, self.mid, self.plane_in, self.depth_in = place, source, mid, plane_in, depth_in
        self.pss, self.prs, self.dss, self.drs = sems

    def plane_copy(self, d):
        p = self.p
        device = lax.rem(p.col + d, PLANE)
        return pltpu.make_async_remote_copy(
            self.source(device), self.plane_in.at[d], self.pss.at[d], self.prs.at[d],
            device_id=(p.row, device), device_id_type=MESH,
        )

    def depth_copy(self, d):
        p = self.p
        return pltpu.make_async_remote_copy(
            self.mid, self.depth_in.at[d], self.dss.at[d], self.drs.at[d],
            device_id=(lax.rem(p.row + d, DEPTH), p.col), device_id_type=MESH,
        )

    def begin(self):
        pl.loop(1, PLANE)(lambda d: self.plane_copy(d).start())

    def middle(self, own):
        pl.loop(1, PLANE)(lambda d: self.plane_copy(d).wait_recv())
        total = own
        for d in range(1, PLANE):
            total = total + self.plane_in[d]
        self.mid[...] = total
        pl.loop(1, DEPTH)(lambda d: self.depth_copy(d).start())

    def end(self):
        pl.loop(1, DEPTH)(lambda d: self.depth_copy(d).wait_recv())
        total = self.mid[...]
        for d in range(1, DEPTH):
            total = total + self.depth_in[d]
        return total

    def drain(self):
        pl.loop(1, PLANE)(lambda d: self.plane_copy(d).wait_send())
        pl.loop(1, DEPTH)(lambda d: self.depth_copy(d).wait_send())


def kernel(
    diag_hbm, pairs_hbm, pattern, newton_diag_hbm, newton_pairs_hbm, warm_hbm, targets,
    out, hess,
    tiles, newton_tiles, xh, xl, nh, nl,
    gw, gr, gq,
    term0, term1, other0, other1,
    fo0, fi0, mo0, mi0, lo0, li0,
    fo1, fi1, mo1, mi1, lo1, li1,
    names_out, names_in, names,
    unit, padded, padded_image, hpad,
    tile0, tile1, mids, plane_in, depth_in,
    load_sems, name_sems,
    ag_ss, ag_rs, rs_ss, rs_rs, pss, prs, dss, drs,
):
    p = Place()
    loads = [
        pltpu.make_async_copy(warm_hbm.at[0], gw.at[p.col], load_sems.at[0]),
        pltpu.make_async_copy(pairs_hbm.at[0], tiles.at[pl.ds(0, K)], load_sems.at[1]),
        pltpu.make_async_copy(diag_hbm.at[0], tiles.at[K], load_sems.at[2]),
        pltpu.make_async_copy(newton_pairs_hbm.at[0], newton_tiles.at[pl.ds(0, K)], load_sems.at[3]),
        pltpu.make_async_copy(newton_diag_hbm.at[0], newton_tiles.at[K], load_sems.at[4]),
    ]
    for load in loads:
        load.start()

    barrier = pltpu.get_barrier_semaphore()

    @pl.loop(1, PLANE)
    def _(d):
        pl.semaphore_signal(barrier, inc=1, device_id=(p.row, lax.rem(p.col + d, PLANE)), device_id_type=MESH)

    @pl.loop(1, DEPTH)
    def _(d):
        pl.semaphore_signal(barrier, inc=1, device_id=(lax.rem(p.row + d, DEPTH), p.col), device_id_type=MESH)

    first_col = p.row * PLANE
    lane = lax.broadcasted_iota(I32, (8, 128), 1)
    table = jnp.full((8, 128), -1, I32)
    for k in range(K):
        table = jnp.where(lane == k, pattern[0, k], table)
    names_out[...] = table
    for g in (gw, gr, gq):
        g[ZERO_BLOCK] = jnp.zeros((C, B), F32)
    for t in (term0, term1, other0, other1):
        t[ZERO_TERM] = jnp.zeros((C, B), F32)

    loads[0].wait()
    pl.semaphore_wait(barrier, PLANE + DEPTH - 2)

    def own(k):
        return pattern[0, k] - first_col

    def theirs(k):
        return names[0, k] - first_col

    def pick(k):
        inside = jnp.clip(pattern[0, k] - first_col, 0, PLANE - 1)
        return jnp.where(pattern[0, k] >= 0, inside, ZERO_BLOCK)

    gathers = [Gather(p, g, ag_ss.at[i], ag_rs.at[i]) for i, g in enumerate((gw, gr, gq))]
    scatters = [
        Scatter(p, term0, other0, fo0, fi0, mo0, mi0, lo0, li0, rs_ss.at[0], rs_rs.at[0], own, theirs),
        Scatter(p, term1, other1, fo1, fi1, mo1, mi1, lo1, li1, rs_ss.at[1], rs_rs.at[1], own, theirs),
    ]

    gathers[0].begin()
    name_copy = pltpu.make_async_remote_copy(
        names_out, names_in, name_sems.at[0], name_sems.at[1], device_id=(p.row, p.sibling), device_id_type=MESH
    )
    name_copy.start()

    loads[1].wait()
    loads[2].wait()
    for k in range(K + 1):
        xh[k], xl[k] = split(tiles[k])

    name_copy.wait()
    name_load = pltpu.make_async_copy(names_in, names, name_sems.at[2])
    name_load.start()

    position = lax.broadcasted_iota(I32, (1, B), 1) + (p.row * PLANE + p.col) * B

    def apply_precision(panel, gather, scatter, aside):
        value = panel[p.col]
        for k in range(K):
            scatter.term[k] = product(value, xh[k], xl[k], NN)
            scatter.begin(k)
        aside()
        gather.first()
        scatter.terms()
        scatter.forward()
        scatter.main_free()
        gather.second(0)
        scatter.main_rest()
        gather.second(1)
        gather.second(2)
        gather.third(0)
        gather.second(3)
        gather.third(1)
        scatter.last()
        gather.third(2)
        gather.third(3)
        total = product(value, xh[K], xl[K], NT)
        gather.end()
        for k in range(K):
            total = total + product(panel[pick(k)], xh[k], xl[k], NT)
        return total + scatter.result()

    def first_aside():
        name_load.wait()

        @pl.loop(0, C)
        def _(c):
            unit[pl.ds(c, 1), :] = (position == targets[c]).astype(F32)

    def second_aside():
        loads[3].wait()
        loads[4].wait()
        for k in range(K + 1):
            nh[k], nl[k] = split(newton_tiles[k])

    residual = unit
    product_w = apply_precision(gw, gathers[0], scatters[0], first_aside)
    gr[p.col] = residual[...] - product_w
    gathers[1].begin()
    gq[p.col] = apply_precision(gr, gathers[1], scatters[1], second_aside)
    gathers[2].begin()

    sums = [
        Total(p, source, mids.at[i], plane_in.at[i], depth_in.at[i], (pss.at[i], prs.at[i], dss.at[i], drs.at[i]))
        for i, source in enumerate((lambda _: tile0, lambda _: tile1, lambda device: hpad.at[device]))
    ]
    r, q = gr[p.col], gq[p.col]
    tile = sums_to_rows([(r, r), (r, q)])
    tile0[...] = tile
    sums[0].begin()
    gathers[2].first()
    gathers[2].second(0)
    sums[0].middle(tile)
    for i in (1, 2, 3):
        gathers[2].second(i)
    for i in range(SIDE):
        gathers[2].third(i)
    first_sums = sums[0].end()
    norm, curve = first_sums[0:1], first_sums[1:2]
    step = norm / curve
    step_c = rows_to_columns(jnp.broadcast_to(step, (8, 128)))[:, 0:1]
    rn = gr[p.col] - step_c * gq[p.col]
    total = 0.5 * product(rn, xh[K], xl[K], NT)
    gathers[2].end()
    for k in range(K):
        block = pick(k)
        total = total + product(gr[block] - step_c * gq[block], xh[k], xl[k], NT)
    tile = sums_to_rows([(rn, rn), (rn, 2.0 * total), (rn, gq[p.col])])
    tile1[...] = tile
    sums[1].begin()
    sums[1].middle(tile)
    second_sums = sums[1].end()
    norm_next, inner, cross = second_sums[0:1], second_sums[1:2], second_sums[2:3]
    beta = norm_next / norm
    curve_next = inner + 2.0 * beta * cross + beta * beta * curve
    step_next = norm_next / curve_next
    rows = lax.broadcasted_iota(I32, (8, 128), 0)
    weights = jnp.where(rows == 0, step + step_next * beta + step_next, step_next * step)
    weights_c = rows_to_columns(weights)
    weight_r, weight_q = weights_c[:, 0:1], weights_c[:, 1:2]

    def estimate(block):
        return gw[block] + weight_r * gr[block] - weight_q * gq[block]

    s = estimate(p.col)
    out[0] = s
    image = jnp.zeros((C, B), F32)
    for k in range(K):
        image = image + product(estimate(pick(k)), nh[k], nl[k], NT)
    diag_image = image + product(s, nh[K], nl[K], NT)
    for j in range(PLANE):
        padded[pl.ds(8 * j, 3)] = s[3 * j : 3 * j + 3]
        padded_image[pl.ds(8 * j, 3)] = image[3 * j : 3 * j + 3]
        padded[pl.ds(8 * j + 3, 5)] = jnp.zeros((5, B), F32)
        padded_image[pl.ds(8 * j + 3, 5)] = jnp.zeros((5, B), F32)
    fill = jnp.zeros((128 - C, B), F32)
    h = lax.dot_general(
        padded[...], jnp.concatenate([diag_image, fill], axis=0), NT, precision=HIGHEST, preferred_element_type=F32
    ) + lax.dot_general(
        padded_image[...], jnp.concatenate([s, fill], axis=0), NT, precision=HIGHEST, preferred_element_type=F32
    )
    for j in range(PLANE):
        hpad[j] = h[8 * j : 8 * j + 8]
    sums[2].begin()
    sums[2].middle(hpad[p.col])
    for g in gathers:
        g.drain()
    for g in scatters:
        g.drain()
    for total in sums[:2]:
        total.drain()
    block_sum = sums[2].end()
    sums[2].drain()
    row_index = lax.broadcasted_iota(I32, (16, 128), 0)
    lane_index = lax.broadcasted_iota(I32, (16, 128), 1)
    chooser = (lane_index == row_index + (C // DEPTH) * p.row).astype(F32)
    picked = lax.dot_general(chooser, block_sum, NT, precision=HIGHEST, preferred_element_type=F32)
    hess[...] = picked[0 : C // DEPTH, 0 : C // PLANE]


def on_device(precision_diag, precision_pairs, pattern_cols, newton_diag, newton_pairs, warm_start, target_rows):
    block = (C, B)
    hbm = pl.BlockSpec(memory_space=pl.ANY)
    smem = pl.BlockSpec(memory_space=pltpu.SMEM)
    vmem = pl.BlockSpec(memory_space=pltpu.VMEM)
    panel = pltpu.VMEM((PLANE + 1,) + block, F32)
    terms = pltpu.VMEM((K + 1,) + block, F32)
    pair_of = pltpu.VMEM((2, 2) + block, F32)
    eight = pltpu.VMEM((2, SIDE) + block, F32)
    steps = [pair_of, pair_of, eight, eight, pltpu.VMEM((SIDE,) + block, F32), pltpu.VMEM((SIDE - 1,) + block, F32)]
    dma = pltpu.SemaphoreType.DMA
    return pl.pallas_call(
        kernel,
        out_shape=(jax.ShapeDtypeStruct((1, C, B), F32), jax.ShapeDtypeStruct((C // DEPTH, C // PLANE), F32)),
        in_specs=[hbm, hbm, smem, hbm, hbm, hbm, smem],
        out_specs=(vmem, vmem),
        scratch_shapes=[
            pltpu.VMEM((K + 1, B, B), F32), pltpu.VMEM((K + 1, B, B), F32),
            pltpu.VMEM((K + 1, B, B), BF16), pltpu.VMEM((K + 1, B, B), BF16),
            pltpu.VMEM((K + 1, B, B), BF16), pltpu.VMEM((K + 1, B, B), BF16),
            panel, panel, panel,
            terms, terms, terms, terms,
            *steps, *steps,
            pltpu.VMEM((8, 128), I32), pltpu.VMEM((8, 128), I32), pltpu.SMEM((8, 128), I32),
            pltpu.VMEM(block, F32), pltpu.VMEM((8 * PLANE, B), F32), pltpu.VMEM((8 * PLANE, B), F32),
            pltpu.VMEM((PLANE, 8, 128), F32),
            pltpu.VMEM((8, 128), F32), pltpu.VMEM((8, 128), F32), pltpu.VMEM((3, 8, 128), F32),
            pltpu.VMEM((3, PLANE, 8, 128), F32), pltpu.VMEM((3, DEPTH, 8, 128), F32),
            dma((5,)), dma((3,)),
            dma((3, N_AG)), dma((3, N_AG)), dma((2, N_RS)), dma((2, N_RS)),
            dma((3, PLANE)), dma((3, PLANE)), dma((3, DEPTH)), dma((3, DEPTH)),
        ],
        compiler_params=pltpu.CompilerParams(
            collective_id=0, has_side_effects=True, vmem_limit_bytes=58 * 2**20
        ),
    )(precision_diag, precision_pairs, pattern_cols, newton_diag, newton_pairs, warm_start, target_rows)


def solution(mesh):
    both = ("row", "col")
    placed = (
        P(both, None, None),
        P(both, None, None, None),
        P(both, None),
        P(both, None, None),
        P(both, None, None, None),
        P(both, None, None),
        P(),
    )
    return jax.shard_map(
        on_device,
        mesh=mesh,
        in_specs=placed,
        out_specs=(P(both, None, None), P("row", "col")),
        check_vma=False,
    )
```

```python
import jax
import jax.numpy as jnp
from jax import lax
from jax.experimental import pallas as pl
from jax.experimental.pallas import tpu as pltpu
from jax.sharding import PartitionSpec as P

HIGHEST = lax.Precision.HIGHEST
MESH = pl.DeviceIdType.MESH
F32, BF16, I32 = jnp.float32, jnp.bfloat16, jnp.int32
C, B, K = 96, 256, 7
PARTS = 2
W = C // PARTS
HALF = W // 2
PLANE, DEPTH, SIDE = 32, 8, 4
NT = (((1,), (1,)), ((), ()))
NN = (((1,), (0,)), ((), ()))
OFFS = (0, -1, 1, 2)
ZERO_BLOCK = PLANE
ZERO_TERM = K
N_AG, N_RS = 35, 14


def split(v):
    high = v.astype(BF16)
    return high, (v - high.astype(F32)).astype(BF16)


def product(v, high_tile, low_tile, dims):
    high, low = split(v)
    both = lax.dot_general(
        jnp.concatenate([high, low], axis=0), high_tile, dims, preferred_element_type=F32
    )
    rest = lax.dot_general(high, low_tile, dims, preferred_element_type=F32)
    return both[: v.shape[0]] + both[v.shape[0] :] + rest


def sums_to_rows(parts):
    lane = lax.broadcasted_iota(I32, (W, 128), 1)
    stack = []
    for pairs in parts:
        wide = jnp.zeros((W, 128), F32)
        for i, (first, second) in enumerate(pairs):
            wide = jnp.where(lane == i, jnp.sum(first * second, axis=1, keepdims=True), wide)
        stack.append(wide)
    stack.append(jnp.zeros((128 - C, 128), F32))
    return jnp.transpose(jnp.concatenate(stack, axis=0))[0:8]


def rows_to_columns(tile):
    wide = jnp.concatenate([tile, jnp.zeros((120, 128), F32)], axis=0)
    return jnp.transpose(wide)[0:C]


class Place:
    def __init__(self):
        self.row = lax.axis_index("row")
        self.col = lax.axis_index("col")
        col = self.col
        self.core = lax.rem(col, 2)
        x, y = lax.rem(col // 2, SIDE), col // (2 * SIDE)
        core = self.core
        self.a, self.b = x + core * (y - x), y + core * (x - y)
        self.sa, self.sb = 2 + 6 * core, 8 - 6 * core
        self.sibling = col + 1 - 2 * core

    def block(self, da, db):
        return (
            lax.rem(self.a + da + SIDE, SIDE) * self.sa
            + lax.rem(self.b + db + SIDE, SIDE) * self.sb
            + self.core
        )

    def sibling_block(self, da, db):
        return (
            lax.rem(self.b + da + SIDE, SIDE) * self.sb
            + lax.rem(self.a + db + SIDE, SIDE) * self.sa
            + (1 - self.core)
        )


class Gather:
    def __init__(self, place, panel, send_sems, recv_sems):
        self.p, self.panel, self.ss, self.rs = place, panel, send_sems, recv_sems
        self.sent = []

    def copy(self, slot, device, index, half=None):
        part = self.panel.at[slot] if half is None else self.panel.at[slot, pl.ds(half * HALF, HALF)]
        return pltpu.make_async_remote_copy(
            part, part, self.ss.at[index], self.rs.at[index], device_id=(self.p.row, device), device_id_type=MESH
        )

    def send(self, *args):
        copy = self.copy(*args)
        copy.start()
        self.sent.append(copy)

    def wait(self, slot, index, half=None):
        self.copy(slot, self.p.sibling, index, half).wait_recv()

    def along_b(self, i):
        p = self.p
        slot = p.block(OFFS[i], 0)
        self.send(slot, p.block(0, 1), 3 + 2 * i)
        self.send(slot, p.block(0, -1), 4 + 2 * i)
        self.send(slot, p.sibling, 19 + 4 * i)

    def begin(self):
        p = self.p
        for n, da in enumerate((1, -1, 2)):
            self.send(p.col, p.block(da, 0), n)
        self.along_b(0)

    def first(self):
        for i in (1, 2, 3):
            self.wait(self.p.block(OFFS[i], 0), i - 1)
            self.along_b(i)

    def second(self, i):
        p = self.p
        for side, db in ((0, -1), (1, 1)):
            slot = p.block(OFFS[i], db)
            self.wait(slot, 3 + 2 * i + side)
            self.send(slot, p.block(0, -db), 11 + 2 * i + side, side)
            self.send(slot, p.sibling, 20 + 4 * i + side)

    def third(self, i):
        slot = self.p.block(OFFS[i], 2)
        for side in (0, 1):
            self.wait(slot, 11 + 2 * i + side, side)
        self.send(slot, self.p.sibling, 22 + 4 * i)

    def end(self):
        for i in range(SIDE):
            for j in range(SIDE):
                self.wait(self.p.sibling_block(OFFS[i], OFFS[j]), 19 + 4 * i + j)

    def drain(self):
        for copy in self.sent:
            copy.wait_send()


class Scatter:
    def __init__(self, place, term, other, fwd_out, fwd_in, main_out, main_in, last_out, last_in, ss, rs, own, theirs):
        self.p, self.term, self.other = place, term, other
        self.fwd_out, self.fwd_in = fwd_out, fwd_in
        self.main_out, self.main_in = main_out, main_in
        self.last_out, self.last_in = last_out, last_in
        self.ss, self.rs, self.own, self.theirs = ss, rs, own, theirs
        self.sent = []

    def copy(self, src, dst, device, index):
        return pltpu.make_async_remote_copy(
            src, dst, self.ss.at[index], self.rs.at[index], device_id=(self.p.row, device), device_id_type=MESH
        )

    def send(self, *args):
        copy = self.copy(*args)
        copy.start()
        self.sent.append(copy)

    def arrived(self, ref, index):
        self.copy(ref, ref, self.p.sibling, index).wait_recv()

    def begin(self):
        every = pl.ds(0, K)
        self.send(self.term.at[every], self.other.at[every], self.p.sibling, 0)

    def share(self, da, db):
        block = self.p.block(da, db)
        return self.term[self.own[block]] + self.other[self.theirs[block]]

    def forward(self):
        p = self.p
        self.arrived(self.other.at[pl.ds(0, K)], 0)
        for side, da in ((0, 1), (1, -1)):
            for j in (0, 1):
                self.fwd_out[side, j] = self.share(2, OFFS[2 * side + j])
            self.send(self.fwd_out.at[side], self.fwd_in.at[side], p.block(da, 0), 1 + side)

    def main(self, side, j, extra=None):
        da = 1 - 2 * side
        value = self.share(da, OFFS[j])
        if extra is not None:
            value = value + self.fwd_in[side, extra]
        self.main_out[side, j] = value
        self.send(self.main_out.at[side, j], self.main_in.at[side, j], self.p.block(da, 0), 3 + SIDE * side + j)

    def main_free(self):
        for j in (0, 1):
            self.main(0, 2 + j)
            self.main(1, j)

    def main_rest(self):
        for side in (0, 1):
            self.arrived(self.fwd_in.at[side], 1 + side)
            for j in (0, 1):
                self.main(side, 2 * side + j, j)

    def last(self):
        for j in (2, 1, 3, 0):
            for side in (0, 1):
                self.arrived(self.main_in.at[side, j], 3 + SIDE * side + j)
            self.last_out[j] = self.share(0, OFFS[j]) + self.main_in[0, j] + self.main_in[1, j]
            if j:
                self.send(self.last_out.at[j], self.last_in.at[j - 1], self.p.block(0, OFFS[j]), 10 + j)

    def result(self):
        for j in (1, 2, 3):
            self.arrived(self.last_in.at[j - 1], 10 + j)
        return self.last_out[0] + self.last_in[0] + self.last_in[1] + self.last_in[2]

    def drain(self):
        for copy in self.sent:
            copy.wait_send()


class Total:
    def __init__(self, place, source, mid, plane_in, depth_in, sems):
        self.p, self.source, self.mid, self.plane_in, self.depth_in = place, source, mid, plane_in, depth_in
        self.pss, self.prs, self.dss, self.drs = sems

    def plane_copy(self, d):
        p = self.p
        device = lax.rem(p.col + d, PLANE)
        return pltpu.make_async_remote_copy(
            self.source(device), self.plane_in.at[d], self.pss.at[d], self.prs.at[d],
            device_id=(p.row, device), device_id_type=MESH,
        )

    def depth_copy(self, d):
        p = self.p
        return pltpu.make_async_remote_copy(
            self.mid, self.depth_in.at[d], self.dss.at[d], self.drs.at[d],
            device_id=(lax.rem(p.row + d, DEPTH), p.col), device_id_type=MESH,
        )

    def begin(self):
        pl.loop(1, PLANE)(lambda d: self.plane_copy(d).start())

    def middle(self, own):
        pl.loop(1, PLANE)(lambda d: self.plane_copy(d).wait_recv())
        total = own
        for d in range(1, PLANE):
            total = total + self.plane_in[d]
        self.mid[...] = total
        pl.loop(1, DEPTH)(lambda d: self.depth_copy(d).start())

    def end(self):
        pl.loop(1, DEPTH)(lambda d: self.depth_copy(d).wait_recv())
        total = self.mid[...]
        for d in range(1, DEPTH):
            total = total + self.depth_in[d]
        return total

    def drain(self):
        pl.loop(1, PLANE)(lambda d: self.plane_copy(d).wait_send())
        pl.loop(1, DEPTH)(lambda d: self.depth_copy(d).wait_send())


def kernel(
    diag_hbm, pairs_hbm, pattern, newton_diag_hbm, newton_pairs_hbm, warm_hbm, targets,
    out, hess,
    tiles, newton_tiles, xh, xl, nh, nl,
    gw0, gw1, gr0, gr1, gq0, gq1,
    *refs,
):
    refs = list(refs)
    n_scatter = 2 * PARTS
    buffers = [[refs.pop(0) for _ in range(8)] for _ in range(n_scatter)]
    (
        names_out, names_in, names, own_table, sibling_table,
        unit, padded, padded_image, right, right_image, message,
        tile, tile_mid, message_mid, tile_plane, tile_depth, message_plane, message_depth,
        load_sems, name_sems,
        ag_ss, ag_rs, rs_ss, rs_rs, pss, prs, dss, drs,
    ) = refs
    p = Place()
    loads = [
        pltpu.make_async_copy(warm_hbm.at[0, pl.ds(0, W)], gw0.at[p.col], load_sems.at[0]),
        pltpu.make_async_copy(warm_hbm.at[0, pl.ds(W, W)], gw1.at[p.col], load_sems.at[5]),
        pltpu.make_async_copy(pairs_hbm.at[0], tiles.at[pl.ds(0, K)], load_sems.at[1]),
        pltpu.make_async_copy(diag_hbm.at[0], tiles.at[K], load_sems.at[2]),
        pltpu.make_async_copy(newton_pairs_hbm.at[0], newton_tiles.at[pl.ds(0, K)], load_sems.at[3]),
        pltpu.make_async_copy(newton_diag_hbm.at[0], newton_tiles.at[K], load_sems.at[4]),
    ]
    for load in loads:
        load.start()

    barrier = pltpu.get_barrier_semaphore()

    @pl.loop(1, PLANE)
    def _(d):
        pl.semaphore_signal(barrier, inc=1, device_id=(p.row, lax.rem(p.col + d, PLANE)), device_id_type=MESH)

    @pl.loop(1, DEPTH)
    def _(d):
        pl.semaphore_signal(barrier, inc=1, device_id=(lax.rem(p.row + d, DEPTH), p.col), device_id_type=MESH)

    first_col = p.row * PLANE

    def fill_table(table, source):
        @pl.loop(0, PLANE)
        def _(block):
            at = jnp.int32(ZERO_TERM)
            for k in range(K):
                at = jnp.where(source[0, k] - first_col == block, k, at)
            table[block] = at

    lane = lax.broadcasted_iota(I32, (8, 128), 1)
    table = jnp.full((8, 128), -1, I32)
    for k in range(K):
        table = jnp.where(lane == k, pattern[0, k], table)
    names_out[...] = table
    panels = ((gw0, gw1), (gr0, gr1), (gq0, gq1))
    for pair in panels:
        for g in pair:
            g[ZERO_BLOCK] = jnp.zeros((W, B), F32)
    for group in buffers:
        for t in group[:2]:
            t[ZERO_TERM] = jnp.zeros((W, B), F32)
    fill_table(own_table, pattern)
    position = lax.broadcasted_iota(I32, (1, B), 1) + (p.row * PLANE + p.col) * B

    @pl.loop(0, C)
    def _(c):
        unit[pl.ds(c, 1), :] = (position == targets[c]).astype(F32)

    for load in loads[:4]:
        load.wait()
    for k in range(K + 1):
        xh[k], xl[k] = split(tiles[k])

    pl.semaphore_wait(barrier, PLANE + DEPTH - 2)

    def pick(k):
        inside = jnp.clip(pattern[0, k] - first_col, 0, PLANE - 1)
        return jnp.where(pattern[0, k] >= 0, inside, ZERO_BLOCK)

    gathers = [
        [Gather(p, panels[v][h], ag_ss.at[v * PARTS + h], ag_rs.at[v * PARTS + h]) for h in range(PARTS)]
        for v in range(3)
    ]
    scatters = [
        [
            Scatter(p, *buffers[v * PARTS + h], rs_ss.at[v * PARTS + h], rs_rs.at[v * PARTS + h], own_table, sibling_table)
            for h in range(PARTS)
        ]
        for v in range(2)
    ]

    def begin(v, h):
        gathers[v][h].begin()
        if v < 2:
            scatter = scatters[v][h]
            value = panels[v][h][p.col]
            for k in range(K):
                scatter.term[k] = product(value, xh[k], xl[k], NN)
            scatter.begin()

    def first(v, h):
        if v < 2:
            scatters[v][h].forward()
            scatters[v][h].main_free()
        gathers[v][h].first()

    def second(v, h):
        if v < 2:
            scatters[v][h].main_rest()
        for i in range(SIDE):
            gathers[v][h].second(i)

    def third(v, h):
        if v < 2:
            scatters[v][h].last()
        for i in range(SIDE):
            gathers[v][h].third(i)

    def image(v, h):
        panel = panels[v][h]
        total = lax.dot_general(panel[p.col], tiles[K], NT, precision=HIGHEST, preferred_element_type=F32)
        gathers[v][h].end()
        for k in range(K):
            total = total + product(panel[pick(k)], xh[k], xl[k], NT)
        return total + scatters[v][h].result()

    def residual(h):
        panels[1][h][p.col] = unit[h * W : (h + 1) * W] - image(0, h)

    def q_image(h):
        panels[2][h][p.col] = image(1, h)

    gathers[0][0].begin()
    name_copy = pltpu.make_async_remote_copy(
        names_out, names_in, name_sems.at[0], name_sems.at[1], device_id=(p.row, p.sibling), device_id_type=MESH
    )
    name_copy.start()
    scatter = scatters[0][0]
    value = gw0[p.col]
    for k in range(K):
        scatter.term[k] = product(value, xh[k], xl[k], NN)
    scatter.begin()
    name_copy.wait()
    name_load = pltpu.make_async_copy(names_in, names, name_sems.at[2])
    name_load.start()
    name_load.wait()
    fill_table(sibling_table, names)

    first(0, 0)
    begin(0, 1)
    second(0, 0)
    first(0, 1)
    third(0, 0)
    second(0, 1)
    residual(0)
    begin(1, 0)
    third(0, 1)
    first(1, 0)
    residual(1)
    begin(1, 1)
    second(1, 0)
    first(1, 1)
    third(1, 0)
    loads[4].wait()
    loads[5].wait()
    for k in range(K + 1):
        nh[k], nl[k] = split(newton_tiles[k])
    second(1, 1)
    q_image(0)
    begin(2, 0)
    third(1, 1)
    first(2, 0)
    q_image(1)
    begin(2, 1)

    sums = Total(p, lambda _: tile, tile_mid, tile_plane, tile_depth, (pss.at[0], prs.at[0], dss.at[0], drs.at[0]))
    pairs = []
    for h in range(PARTS):
        r, q = panels[1][h][p.col], panels[2][h][p.col]
        pairs.append([(r, r), (r, q), (q, q)])
    own_sums = sums_to_rows(pairs)
    tile[...] = own_sums
    sums.begin()
    second(2, 0)
    first(2, 1)
    sums.middle(own_sums)
    third(2, 0)
    second(2, 1)
    totals = sums.end()
    norm, curve, square = totals[0:1], totals[1:2], totals[2:3]
    step = norm / curve
    norm_next = step * step * square - 2.0 * step * curve + norm
    beta = norm_next / norm
    rows = lax.broadcasted_iota(I32, (8, 128), 0)
    weights = rows_to_columns(jnp.where(rows == 0, step, beta))

    def weight(h):
        part = weights[h * W : (h + 1) * W]
        return part[:, 0:1], 1.0 + part[:, 1:2]

    def estimate(h, block):
        return gw(h)[block] + weight(h)[0] * gr(h)[block]

    def direction(h, block):
        step_c, scale = weight(h)
        return scale * gr(h)[block] - step_c * gq(h)[block]

    def gw(h):
        return panels[0][h]

    def gr(h):
        return panels[1][h]

    def gq(h):
        return panels[2][h]

    def both_parts(f, block):
        return jnp.concatenate([f(h, block) for h in range(PARTS)], axis=0)

    estimate_image = jnp.zeros((C, B), F32)
    for k in range(K):
        estimate_image = estimate_image + product(both_parts(estimate, pick(k)), nh[k], nl[k], NT)
    u = both_parts(estimate, p.col)
    estimate_full = estimate_image + product(u, nh[K], nl[K], NT)
    third(2, 1)
    for h in range(PARTS):
        gathers[2][h].end()

    d = both_parts(direction, p.col)
    half_image = 0.5 * product(d, xh[K], xl[K], NT)
    direction_image = jnp.zeros((C, B), F32)
    for k in range(K):
        picked = both_parts(direction, pick(k))
        half_image = half_image + product(picked, xh[k], xl[k], NT)
        direction_image = direction_image + product(picked, nh[k], nl[k], NT)
    direction_full = direction_image + product(d, nh[K], nl[K], NT)
    curve_next = sums_to_rows([[(d[h * W : (h + 1) * W], 2.0 * half_image[h * W : (h + 1) * W])] for h in range(PARTS)])

    for j in range(PLANE):
        rows3 = slice(3 * j, 3 * j + 3)
        for ref, first_half, second_half in ((padded, u, d), (padded_image, estimate_image, direction_image)):
            ref[pl.ds(8 * j, 3)] = first_half[rows3]
            ref[pl.ds(8 * j + 3, 3)] = second_half[rows3]
            ref[pl.ds(8 * j + 6, 2)] = jnp.zeros((2, B), F32)
    fill = jnp.zeros((128 - C, B), F32)
    right[...] = jnp.concatenate([u, fill, d, fill], axis=0)
    right_image[...] = jnp.concatenate([estimate_full, fill, direction_full, fill], axis=0)
    pair_sums = lax.dot_general(
        padded[...], right_image[...], NT, precision=HIGHEST, preferred_element_type=F32
    ) + lax.dot_general(padded_image[...], right[...], NT, precision=HIGHEST, preferred_element_type=F32)
    curve_row = jnp.concatenate([curve_next[0:1], jnp.zeros((1, 128), F32)], axis=1)
    row_of = lax.broadcasted_iota(I32, (8, 256), 0)
    for j in range(PLANE):
        message[j] = jnp.where(row_of == 6, curve_row, pair_sums[8 * j : 8 * j + 8])
    last = Total(
        p, lambda device: message.at[device], message_mid, message_plane, message_depth,
        (pss.at[1], prs.at[1], dss.at[1], drs.at[1]),
    )
    last.begin()
    for v in range(3):
        for h in range(PARTS):
            gathers[v][h].drain()
            if v < 2:
                scatters[v][h].drain()
    sums.drain()
    last.middle(message[p.col])
    total = last.end()
    last.drain()
    step_next = norm_next / total[6:7, 0:128]
    spread = rows_to_columns(jnp.broadcast_to(step_next, (8, 128)))
    out[0] = u + spread[:, 0:1] * d
    lane8 = lax.broadcasted_iota(I32, (8, 128), 1)
    row8 = lax.broadcasted_iota(I32, (8, 128), 0)
    mine = lane8 == row8 + (C // PLANE) * p.col
    step_rows = jnp.sum(jnp.where(mine, step_next, 0.0), axis=1, keepdims=True)[0:3]
    block_rows = total[0:3, 0:128] + step_next * total[0:3, 128:256]
    block_rows = block_rows + step_rows * (total[3:6, 0:128] + step_next * total[3:6, 128:256])
    block_rows = jnp.where(lane8[0:3] < C, block_rows, 0.0)
    block_rows = jnp.concatenate([block_rows, jnp.zeros((5, 128), F32)], axis=0)
    row_index = lax.broadcasted_iota(I32, (16, 128), 0)
    lane_index = lax.broadcasted_iota(I32, (16, 128), 1)
    chooser = (lane_index == row_index + (C // DEPTH) * p.row).astype(F32)
    picked = lax.dot_general(chooser, block_rows, NT, precision=HIGHEST, preferred_element_type=F32)
    hess[...] = picked[0 : C // DEPTH, 0 : C // PLANE]


def on_device(precision_diag, precision_pairs, pattern_cols, newton_diag, newton_pairs, warm_start, target_rows):
    block = (W, B)
    hbm = pl.BlockSpec(memory_space=pl.ANY)
    smem = pl.BlockSpec(memory_space=pltpu.SMEM)
    vmem = pl.BlockSpec(memory_space=pltpu.VMEM)
    panel = pltpu.VMEM((PLANE + 1,) + block, F32)
    terms = pltpu.VMEM((K + 1,) + block, F32)
    pair_of = pltpu.VMEM((2, 2) + block, F32)
    eight = pltpu.VMEM((2, SIDE) + block, F32)
    four, three = pltpu.VMEM((SIDE,) + block, F32), pltpu.VMEM((SIDE - 1,) + block, F32)
    scatter = [terms, terms, pair_of, pair_of, eight, eight, four, three]
    square = pltpu.VMEM((8 * PLANE, B), F32)
    tile, message = (8, 128), (8, 256)
    dma = pltpu.SemaphoreType.DMA
    return pl.pallas_call(
        kernel,
        out_shape=(jax.ShapeDtypeStruct((1, C, B), F32), jax.ShapeDtypeStruct((C // DEPTH, C // PLANE), F32)),
        in_specs=[hbm, hbm, smem, hbm, hbm, hbm, smem],
        out_specs=(vmem, vmem),
        scratch_shapes=[
            pltpu.VMEM((K + 1, B, B), F32), pltpu.VMEM((K + 1, B, B), F32),
            pltpu.VMEM((K + 1, B, B), BF16), pltpu.VMEM((K + 1, B, B), BF16),
            pltpu.VMEM((K + 1, B, B), BF16), pltpu.VMEM((K + 1, B, B), BF16),
            *[panel] * (3 * PARTS),
            *scatter * (2 * PARTS),
            pltpu.VMEM((8, 128), I32), pltpu.VMEM((8, 128), I32), pltpu.SMEM((8, 128), I32),
            pltpu.SMEM((PLANE,), I32), pltpu.SMEM((PLANE,), I32),
            pltpu.VMEM((C, B), F32), square, square, square, square,
            pltpu.VMEM((PLANE,) + message, F32),
            pltpu.VMEM(tile, F32), pltpu.VMEM(tile, F32), pltpu.VMEM(message, F32),
            pltpu.VMEM((PLANE,) + tile, F32), pltpu.VMEM((DEPTH,) + tile, F32),
            pltpu.VMEM((PLANE,) + message, F32), pltpu.VMEM((DEPTH,) + message, F32),
            dma((6,)), dma((3,)),
            dma((3 * PARTS, N_AG)), dma((3 * PARTS, N_AG)), dma((2 * PARTS, N_RS)), dma((2 * PARTS, N_RS)),
            dma((2, PLANE)), dma((2, PLANE)), dma((2, DEPTH)), dma((2, DEPTH)),
        ],
        compiler_params=pltpu.CompilerParams(
            collective_id=0, has_side_effects=True, vmem_limit_bytes=58 * 2**20
        ),
    )(precision_diag, precision_pairs, pattern_cols, newton_diag, newton_pairs, warm_start, target_rows)


def solution(mesh):
    both = ("row", "col")
    placed = (
        P(both, None, None),
        P(both, None, None, None),
        P(both, None),
        P(both, None, None),
        P(both, None, None, None),
        P(both, None, None),
        P(),
    )
    return jax.shard_map(
        on_device,
        mesh=mesh,
        in_specs=placed,
        out_specs=(P(both, None, None), P("row", "col")),
        check_vma=False,
    )
```

```python
import jax
import jax.numpy as jnp
from jax import lax
from jax.experimental import pallas as pl
from jax.experimental.pallas import tpu as pltpu
from jax.sharding import PartitionSpec as P

HIGHEST = lax.Precision.HIGHEST
MESH = pl.DeviceIdType.MESH
F32, BF16, I32 = jnp.float32, jnp.bfloat16, jnp.int32
C, B, K = 96, 256, 7
PARTS = 2
W = C // PARTS
HALF = W // 2
PLANE, DEPTH, SIDE = 32, 8, 4
NT = (((1,), (1,)), ((), ()))
NN = (((1,), (0,)), ((), ()))
OFFS = (0, -1, 1, 2)
ZERO_BLOCK = PLANE
ZERO_TERM = K
N_AG, N_RS = 12, 7


def split(v):
    high = v.astype(BF16)
    return high, (v - high.astype(F32)).astype(BF16)


def product(v, high_tile, low_tile, dims):
    high, low = split(v)
    both = lax.dot_general(
        jnp.concatenate([high, low], axis=0), high_tile, dims, preferred_element_type=F32
    )
    rest = lax.dot_general(high, low_tile, dims, preferred_element_type=F32)
    return both[: v.shape[0]] + both[v.shape[0] :] + rest


def side_sums(pairs):
    n = pairs[0][0].shape[0]
    lane = lax.broadcasted_iota(I32, (n, 128), 1)
    wide = jnp.zeros((n, 128), F32)
    for i, (first, second) in enumerate(pairs):
        wide = jnp.where(lane == i, jnp.sum(first * second, axis=1, keepdims=True), wide)
    return wide


def stack_to_rows(stack):
    return jnp.transpose(jnp.concatenate(stack + [jnp.zeros((128 - C, 128), F32)], axis=0))[0:8]


def rows_to_columns(tile):
    wide = jnp.concatenate([tile, jnp.zeros((120, 128), F32)], axis=0)
    return jnp.transpose(wide)[0:C]


class Place:
    def __init__(self):
        self.row = lax.axis_index("row")
        self.col = lax.axis_index("col")
        col = self.col
        self.core = lax.rem(col, 2)
        x, y = lax.rem(col // 2, SIDE), col // (2 * SIDE)
        core = self.core
        self.a, self.b = x + core * (y - x), y + core * (x - y)
        self.sa, self.sb = 2 + 6 * core, 8 - 6 * core
        self.sibling = col + 1 - 2 * core

    def block(self, da, db):
        return (
            lax.rem(self.a + da + SIDE, SIDE) * self.sa
            + lax.rem(self.b + db + SIDE, SIDE) * self.sb
            + self.core
        )

    def sibling_block(self, da, db):
        return (
            lax.rem(self.b + da + SIDE, SIDE) * self.sb
            + lax.rem(self.a + db + SIDE, SIDE) * self.sa
            + (1 - self.core)
        )


class Gather:
    def __init__(self, place, panel, send_sem, recv_sems):
        self.p, self.panel, self.ss, self.rs = place, panel, send_sem, recv_sems

    def copy(self, part, device, index):
        return pltpu.make_async_remote_copy(
            part, part, self.ss, self.rs.at[index], device_id=(self.p.row, device), device_id_type=MESH
        )

    def send(self, slot, device, index, half=None):
        part = self.panel.at[slot] if half is None else self.panel.at[slot, pl.ds(half * HALF, HALF)]
        self.copy(part, device, index).start()

    def wait(self, index, blocks):
        self.copy(self.panel.at[pl.ds(0, blocks)], self.p.sibling, index).wait_recv()

    def along_b(self, i):
        p = self.p
        slot = p.block(OFFS[i], 0)
        self.send(slot, p.block(0, 1), 3 + i)
        self.send(slot, p.block(0, -1), 3 + i)
        self.send(slot, p.sibling, 11)

    def begin(self):
        p = self.p
        for n, da in enumerate((1, -1, 2)):
            self.send(p.col, p.block(da, 0), n)
        self.along_b(0)

    def first(self):
        for i in (1, 2, 3):
            self.wait(i - 1, 1)
            self.along_b(i)

    def second(self, i):
        p = self.p
        self.wait(3 + i, 2)
        for half, db in ((0, -1), (1, 1)):
            self.send(p.block(OFFS[i], db), p.block(0, -db), 7 + i, half)
        for db in (-1, 1):
            self.send(p.block(OFFS[i], db), p.sibling, 11)

    def third(self, i):
        self.wait(7 + i, 1)
        self.send(self.p.block(OFFS[i], 2), self.p.sibling, 11)

    def end(self):
        self.wait(11, SIDE * SIDE)

    def drain(self):
        sent = 3 + 2 * SIDE + SIDE + SIDE * SIDE
        self.copy(self.panel.at[pl.ds(0, sent)], self.p.sibling, 11).wait_send()


class Scatter:
    def __init__(self, place, panel, term, other, fwd_out, fwd_in, main_out, main_in, last_out, last_in, ss, rs, own, theirs):
        self.p, self.panel, self.term, self.other = place, panel, term, other
        self.fwd_out, self.fwd_in = fwd_out, fwd_in
        self.main_out, self.main_in = main_out, main_in
        self.last_out, self.last_in = last_out, last_in
        self.ss, self.rs, self.own, self.theirs = ss, rs, own, theirs

    def copy(self, src, dst, device, index):
        return pltpu.make_async_remote_copy(
            src, dst, self.ss, self.rs.at[index], device_id=(self.p.row, device), device_id_type=MESH
        )

    def send(self, *args):
        self.copy(*args).start()

    def wait(self, ref, index):
        self.copy(ref, ref, self.p.sibling, index).wait_recv()

    def begin(self):
        every = pl.ds(0, K)
        self.send(self.term.at[every], self.other.at[every], self.p.sibling, 0)

    def share(self, da, db):
        block = self.p.block(da, db)
        return self.term[self.own[block]] + self.other[self.theirs[block]]

    def forward(self):
        self.wait(self.other.at[pl.ds(0, K)], 0)
        for side, da in ((0, 1), (1, -1)):
            for j in (0, 1):
                self.fwd_out[side, j] = self.share(2, OFFS[2 * side + j])
            self.send(self.fwd_out.at[side], self.fwd_in.at[side], self.p.block(da, 0), 1)

    def main(self, side, j, extra=None):
        da = 1 - 2 * side
        value = self.share(da, OFFS[j])
        if extra is not None:
            value = value + self.fwd_in[side, extra]
        self.main_out[j, side] = value
        self.send(self.main_out.at[j, side], self.main_in.at[j, side], self.p.block(da, 0), 2 + j)

    def main_free(self):
        for j in (0, 1):
            self.main(0, 2 + j)
            self.main(1, j)

    def main_rest(self):
        self.wait(self.fwd_in, 1)
        for j in (0, 1):
            self.main(0, j, j)
            self.main(1, 2 + j, j)

    def last(self):
        for j in (3, 1, 2, 0):
            self.wait(self.main_in.at[j], 2 + j)
            self.last_out[j] = self.share(0, OFFS[j]) + self.main_in[j, 0] + self.main_in[j, 1]
            if j:
                self.send(self.last_out.at[j], self.last_in.at[j - 1], self.p.block(0, OFFS[j]), 6)

    def result(self):
        self.wait(self.last_in, 6)
        return self.last_out[0] + self.last_in[0] + self.last_in[1] + self.last_in[2]

    def drain(self):
        sent = K + 4 + 2 * SIDE + SIDE - 1
        part = self.panel.at[pl.ds(0, sent)]
        self.copy(part, part, self.p.sibling, 6).wait_send()


class Total:
    def __init__(self, place, source, mid, plane_in, depth_in, sems):
        self.p, self.source, self.mid, self.plane_in, self.depth_in = place, source, mid, plane_in, depth_in
        self.pss, self.prs, self.dss, self.drs = sems

    def plane_copy(self, d):
        p = self.p
        device = lax.rem(p.col + d, PLANE)
        return pltpu.make_async_remote_copy(
            self.source(device), self.plane_in.at[d], self.pss, self.prs,
            device_id=(p.row, device), device_id_type=MESH,
        )

    def depth_copy(self, d):
        p = self.p
        return pltpu.make_async_remote_copy(
            self.mid, self.depth_in.at[d], self.dss, self.drs,
            device_id=(lax.rem(p.row + d, DEPTH), p.col), device_id_type=MESH,
        )

    def begin(self):
        pl.loop(1, PLANE)(lambda d: self.plane_copy(d).start())

    def whole(self, ref, count, send_sem, recv_sem):
        part = ref.at[pl.ds(1, count - 1)]
        return pltpu.make_async_remote_copy(
            part, part, send_sem, recv_sem, device_id=(self.p.row, self.p.sibling), device_id_type=MESH
        )

    def plane_whole(self):
        return self.whole(self.plane_in, PLANE, self.pss, self.prs)

    def depth_whole(self):
        return self.whole(self.depth_in, DEPTH, self.dss, self.drs)

    def middle(self, own):
        self.plane_whole().wait_recv()
        total = own
        for d in range(1, PLANE):
            total = total + self.plane_in[d]
        self.mid[...] = total
        pl.loop(1, DEPTH)(lambda d: self.depth_copy(d).start())

    def end(self):
        self.depth_whole().wait_recv()
        total = self.mid[...]
        for d in range(1, DEPTH):
            total = total + self.depth_in[d]
        return total

    def drain(self):
        self.plane_whole().wait_send()
        self.depth_whole().wait_send()


def kernel(
    diag_hbm, pairs_hbm, pattern, newton_diag_hbm, newton_pairs_hbm, warm_hbm, targets,
    out, hess,
    tiles, newton_tiles, xh, xl, nh, nl,
    gw0, gw1, gr0, gr1, gq0, gq1,
    *refs,
):
    refs = list(refs)
    n_scatter = 2 * PARTS
    buffers = [[refs.pop(0) for _ in range(8)] for _ in range(n_scatter)]
    (
        names_out, names_in, names, own_table, sibling_table,
        unit, padded, padded_image, right, right_image, message,
        tile, tile_mid, message_mid, tile_plane, tile_depth, message_plane, message_depth,
        load_sems, name_sems,
        ag_ss, ag_rs, rs_ss, rs_rs, pss, prs, dss, drs,
    ) = refs
    p = Place()
    barrier = pltpu.get_barrier_semaphore()

    @pl.loop(1, PLANE)
    def _(d):
        pl.semaphore_signal(barrier, inc=1, device_id=(p.row, lax.rem(p.col + d, PLANE)), device_id_type=MESH)

    @pl.loop(1, DEPTH)
    def _(d):
        pl.semaphore_signal(barrier, inc=1, device_id=(lax.rem(p.row + d, DEPTH), p.col), device_id_type=MESH)

    loads = [
        pltpu.make_async_copy(warm_hbm.at[0, pl.ds(0, W)], gw0.at[p.col], load_sems.at[0]),
        pltpu.make_async_copy(warm_hbm.at[0, pl.ds(W, W)], gw1.at[p.col], load_sems.at[5]),
        pltpu.make_async_copy(pairs_hbm.at[0], tiles.at[pl.ds(0, K)], load_sems.at[1]),
        pltpu.make_async_copy(diag_hbm.at[0], tiles.at[K], load_sems.at[2]),
        pltpu.make_async_copy(newton_pairs_hbm.at[0], newton_tiles.at[pl.ds(0, K)], load_sems.at[3]),
        pltpu.make_async_copy(newton_diag_hbm.at[0], newton_tiles.at[K], load_sems.at[4]),
    ]
    for load in loads:
        load.start()

    first_col = p.row * PLANE

    def fill_table(table, source):
        @pl.loop(0, PLANE)
        def _(block):
            at = jnp.int32(ZERO_TERM)
            for k in range(K):
                at = jnp.where(source[0, k] - first_col == block, k, at)
            table[block] = at

    lane = lax.broadcasted_iota(I32, (8, 128), 1)
    table = jnp.full((8, 128), -1, I32)
    for k in range(K):
        table = jnp.where(lane == k, pattern[0, k], table)
    names_out[...] = table
    panels = ((gw0, gw1), (gr0, gr1), (gq0, gq1))
    loads[0].wait()
    loads[1].wait()
    pl.semaphore_wait(barrier, PLANE + DEPTH - 2)

    def pick(k):
        inside = jnp.clip(pattern[0, k] - first_col, 0, PLANE - 1)
        return jnp.where(pattern[0, k] >= 0, inside, ZERO_BLOCK)

    gathers = [
        [Gather(p, panels[v][h], ag_ss.at[v * PARTS + h], ag_rs.at[v * PARTS + h]) for h in range(PARTS)]
        for v in range(3)
    ]
    scatters = [
        [
            Scatter(p, panels[v][h], *buffers[v * PARTS + h], rs_ss.at[v * PARTS + h], rs_rs.at[v * PARTS + h], own_table, sibling_table)
            for h in range(PARTS)
        ]
        for v in range(2)
    ]

    def begin(v, h):
        gathers[v][h].begin()
        if v < 2:
            scatter = scatters[v][h]
            value = panels[v][h][p.col]
            for k in range(K):
                scatter.term[k] = product(value, xh[k], xl[k], NN)
            scatter.begin()

    def first(v, h):
        if v < 2:
            scatters[v][h].forward()
            scatters[v][h].main_free()
        gathers[v][h].first()

    def second(v, h):
        if v < 2:
            scatters[v][h].main_rest()
        for i in range(SIDE):
            gathers[v][h].second(i)

    def third(v, h):
        if v < 2:
            scatters[v][h].last()
        for i in range(SIDE):
            gathers[v][h].third(i)

    def image(v, h):
        panel = panels[v][h]
        total = lax.dot_general(panel[p.col], tiles[K], NT, precision=HIGHEST, preferred_element_type=F32)
        gathers[v][h].end()
        for k in range(K):
            total = total + product(panel[pick(k)], xh[k], xl[k], NT)
        return total + scatters[v][h].result()

    def residual(h):
        panels[1][h][p.col] = unit[h * W : (h + 1) * W] - image(0, h)

    def q_image(h):
        panels[2][h][p.col] = image(1, h)

    def both_parts(f, block):
        return jnp.concatenate([f(h, block) for h in range(PARTS)], axis=0)

    def make_units():
        position = lax.broadcasted_iota(I32, (1, B), 1) + (p.row * PLANE + p.col) * B

        @pl.loop(0, C)
        def _(c):
            unit[pl.ds(c, 1), :] = (position == targets[c]).astype(F32)

    def split_newton():
        loads[4].wait()
        loads[5].wait()
        for k in range(K + 1):
            nh[k], nl[k] = split(newton_tiles[k])

    stacks = []

    def own_sums_of(h):
        r, q = panels[1][h][p.col], panels[2][h][p.col]
        stacks.append(side_sums([(r, r), (r, q), (q, q)]))

    gathers[0][0].begin()
    name_copy = pltpu.make_async_remote_copy(
        names_out, names_in, name_sems.at[0], name_sems.at[1], device_id=(p.row, p.sibling), device_id_type=MESH
    )
    name_copy.start()
    gathers[0][1].begin()
    loads[2].wait()
    value = both_parts(lambda h, block: panels[0][h][block], p.col)
    for k in range(K):
        xh[k], xl[k] = split(tiles[k])
        term = product(value, xh[k], xl[k], NN)
        for h in range(PARTS):
            scatters[0][h].term[k] = term[h * W : (h + 1) * W]
    for h in range(PARTS):
        scatters[0][h].begin()
    loads[3].wait()
    xh[K], xl[K] = split(tiles[K])
    for pair in panels:
        for g in pair:
            g[ZERO_BLOCK] = jnp.zeros((W, B), F32)
    for group in buffers:
        for t in group[:2]:
            t[ZERO_TERM] = jnp.zeros((W, B), F32)
    fill_table(own_table, pattern)
    name_copy.wait()
    name_load = pltpu.make_async_copy(names_in, names, name_sems.at[2])
    name_load.start()
    name_load.wait()
    fill_table(sibling_table, names)

    first(0, 0)
    first(0, 1)
    second(0, 0)
    make_units()
    third(0, 0)
    second(0, 1)
    residual(0)
    begin(1, 0)
    third(0, 1)
    first(1, 0)
    residual(1)
    begin(1, 1)
    second(1, 0)
    first(1, 1)
    split_newton()
    third(1, 0)
    second(1, 1)
    q_image(0)
    begin(2, 0)
    third(1, 1)
    first(2, 0)
    own_sums_of(0)
    q_image(1)
    begin(2, 1)

    sums = Total(p, lambda _: tile, tile_mid, tile_plane, tile_depth, (pss.at[0], prs.at[0], dss.at[0], drs.at[0]))
    own_sums_of(1)
    own_sums = stack_to_rows(stacks)
    tile[...] = own_sums
    sums.begin()
    second(2, 0)
    first(2, 1)
    sums.middle(own_sums)
    third(2, 0)
    second(2, 1)
    third(2, 1)
    totals = sums.end()
    norm, curve, square = totals[0:1], totals[1:2], totals[2:3]
    step = norm / curve
    norm_next = step * step * square - 2.0 * step * curve + norm
    beta = norm_next / norm
    rows = lax.broadcasted_iota(I32, (8, 128), 0)
    weights = rows_to_columns(jnp.where(rows == 0, step, beta))

    def weight(h):
        part = weights[h * W : (h + 1) * W]
        return part[:, 0:1], 1.0 + part[:, 1:2]

    def estimate(h, block):
        return gw(h)[block] + weight(h)[0] * gr(h)[block]

    def direction(h, block):
        step_c, scale = weight(h)
        return scale * gr(h)[block] - step_c * gq(h)[block]

    def gw(h):
        return panels[0][h]

    def gr(h):
        return panels[1][h]

    def gq(h):
        return panels[2][h]

    estimate_image = jnp.zeros((C, B), F32)
    for k in range(K):
        estimate_image = estimate_image + product(both_parts(estimate, pick(k)), nh[k], nl[k], NT)
    u = both_parts(estimate, p.col)
    estimate_full = estimate_image + product(u, nh[K], nl[K], NT)
    for h in range(PARTS):
        gathers[2][h].end()

    d = both_parts(direction, p.col)
    half_image = 0.5 * product(d, xh[K], xl[K], NT)
    direction_image = jnp.zeros((C, B), F32)
    for k in range(K):
        picked = both_parts(direction, pick(k))
        half_image = half_image + product(picked, xh[k], xl[k], NT)
        direction_image = direction_image + product(picked, nh[k], nl[k], NT)
    direction_full = direction_image + product(d, nh[K], nl[K], NT)
    curve_next = stack_to_rows([side_sums([(d, 2.0 * half_image)])])

    for j in range(PLANE):
        rows3 = slice(3 * j, 3 * j + 3)
        for ref, first_half, second_half in ((padded, u, d), (padded_image, estimate_image, direction_image)):
            ref[pl.ds(8 * j, 3)] = first_half[rows3]
            ref[pl.ds(8 * j + 3, 3)] = second_half[rows3]
            ref[pl.ds(8 * j + 6, 2)] = jnp.zeros((2, B), F32)
    fill = jnp.zeros((128 - C, B), F32)
    right[...] = jnp.concatenate([u, fill, d, fill], axis=0)
    right_image[...] = jnp.concatenate([estimate_full, fill, direction_full, fill], axis=0)
    pair_sums = lax.dot_general(
        padded[...], right_image[...], NT, precision=HIGHEST, preferred_element_type=F32
    ) + lax.dot_general(padded_image[...], right[...], NT, precision=HIGHEST, preferred_element_type=F32)
    curve_row = jnp.concatenate([curve_next[0:1], jnp.zeros((1, 128), F32)], axis=1)
    row_of = lax.broadcasted_iota(I32, (8, 256), 0)
    for j in range(PLANE):
        message[j] = jnp.where(row_of == 6, curve_row, pair_sums[8 * j : 8 * j + 8])
    last = Total(
        p, lambda device: message.at[device], message_mid, message_plane, message_depth,
        (pss.at[1], prs.at[1], dss.at[1], drs.at[1]),
    )
    last.begin()
    for v in range(3):
        for h in range(PARTS):
            gathers[v][h].drain()
            if v < 2:
                scatters[v][h].drain()
    sums.drain()
    last.middle(message[p.col])
    total = last.end()
    last.drain()
    step_next = norm_next / total[6:7, 0:128]
    spread = rows_to_columns(jnp.broadcast_to(step_next, (8, 128)))
    out[0] = u + spread[:, 0:1] * d
    lane8 = lax.broadcasted_iota(I32, (8, 128), 1)
    row8 = lax.broadcasted_iota(I32, (8, 128), 0)
    mine = lane8 == row8 + (C // PLANE) * p.col
    step_rows = jnp.sum(jnp.where(mine, step_next, 0.0), axis=1, keepdims=True)[0:3]
    block_rows = total[0:3, 0:128] + step_next * total[0:3, 128:256]
    block_rows = block_rows + step_rows * (total[3:6, 0:128] + step_next * total[3:6, 128:256])
    block_rows = jnp.where(lane8[0:3] < C, block_rows, 0.0)
    block_rows = jnp.concatenate([block_rows, jnp.zeros((5, 128), F32)], axis=0)
    row_index = lax.broadcasted_iota(I32, (16, 128), 0)
    lane_index = lax.broadcasted_iota(I32, (16, 128), 1)
    chooser = (lane_index == row_index + (C // DEPTH) * p.row).astype(F32)
    picked = lax.dot_general(chooser, block_rows, NT, precision=HIGHEST, preferred_element_type=F32)
    hess[...] = picked[0 : C // DEPTH, 0 : C // PLANE]


def on_device(precision_diag, precision_pairs, pattern_cols, newton_diag, newton_pairs, warm_start, target_rows):
    block = (W, B)
    hbm = pl.BlockSpec(memory_space=pl.ANY)
    smem = pl.BlockSpec(memory_space=pltpu.SMEM)
    vmem = pl.BlockSpec(memory_space=pltpu.VMEM)
    panel = pltpu.VMEM((PLANE + 1,) + block, F32)
    terms = pltpu.VMEM((K + 1,) + block, F32)
    pair_of = pltpu.VMEM((2, 2) + block, F32)
    eight = pltpu.VMEM((SIDE, 2) + block, F32)
    four, three = pltpu.VMEM((SIDE,) + block, F32), pltpu.VMEM((SIDE - 1,) + block, F32)
    scatter = [terms, terms, pair_of, pair_of, eight, eight, four, three]
    square = pltpu.VMEM((8 * PLANE, B), F32)
    tile, message = (8, 128), (8, 256)
    dma = pltpu.SemaphoreType.DMA
    return pl.pallas_call(
        kernel,
        out_shape=(jax.ShapeDtypeStruct((1, C, B), F32), jax.ShapeDtypeStruct((C // DEPTH, C // PLANE), F32)),
        in_specs=[hbm, hbm, smem, hbm, hbm, hbm, smem],
        out_specs=(vmem, vmem),
        scratch_shapes=[
            pltpu.VMEM((K + 1, B, B), F32), pltpu.VMEM((K + 1, B, B), F32),
            pltpu.VMEM((K + 1, B, B), BF16), pltpu.VMEM((K + 1, B, B), BF16),
            pltpu.VMEM((K + 1, B, B), BF16), pltpu.VMEM((K + 1, B, B), BF16),
            *[panel] * (3 * PARTS),
            *scatter * (2 * PARTS),
            pltpu.VMEM((8, 128), I32), pltpu.VMEM((8, 128), I32), pltpu.SMEM((8, 128), I32),
            pltpu.SMEM((PLANE,), I32), pltpu.SMEM((PLANE,), I32),
            pltpu.VMEM((C, B), F32), square, square, square, square,
            pltpu.VMEM((PLANE,) + message, F32),
            pltpu.VMEM(tile, F32), pltpu.VMEM(tile, F32), pltpu.VMEM(message, F32),
            pltpu.VMEM((PLANE,) + tile, F32), pltpu.VMEM((DEPTH,) + tile, F32),
            pltpu.VMEM((PLANE,) + message, F32), pltpu.VMEM((DEPTH,) + message, F32),
            dma((6,)), dma((3,)),
            dma((3 * PARTS,)), dma((3 * PARTS, N_AG)), dma((2 * PARTS,)), dma((2 * PARTS, N_RS)),
            dma((2,)), dma((2,)), dma((2,)), dma((2,)),
        ],
        compiler_params=pltpu.CompilerParams(
            collective_id=0, has_side_effects=True, vmem_limit_bytes=58 * 2**20
        ),
    )(precision_diag, precision_pairs, pattern_cols, newton_diag, newton_pairs, warm_start, target_rows)


def solution(mesh):
    both = ("row", "col")
    placed = (
        P(both, None, None),
        P(both, None, None, None),
        P(both, None),
        P(both, None, None),
        P(both, None, None, None),
        P(both, None, None),
        P(),
    )
    return jax.shard_map(
        on_device,
        mesh=mesh,
        in_specs=placed,
        out_specs=(P(both, None, None), P("row", "col")),
        check_vma=False,
    )
```

```python
import jax
import jax.numpy as jnp
from jax import lax
from jax.experimental import pallas as pl
from jax.experimental.pallas import tpu as pltpu
from jax.sharding import PartitionSpec as P

HIGHEST = lax.Precision.HIGHEST
MESH = pl.DeviceIdType.MESH
F32, BF16, I32 = jnp.float32, jnp.bfloat16, jnp.int32
C, B, K = 96, 256, 7
PARTS = 2
W = C // PARTS
HALF = W // 2
PLANE, DEPTH, SIDE = 32, 8, 4
NT = (((1,), (1,)), ((), ()))
NN = (((1,), (0,)), ((), ()))
OFFS = (0, -1, 1, 2)
ZERO_BLOCK = PLANE
ZERO_TERM = K
N_AG, N_RS = 12, 7
STRAIGHT = ((2, 1),)


def split(v):
    high = v.astype(BF16)
    return high, (v - high.astype(F32)).astype(BF16)


def product(v, high_tile, low_tile, dims):
    high, low = split(v)
    both = lax.dot_general(
        jnp.concatenate([high, low], axis=0), high_tile, dims, preferred_element_type=F32
    )
    rest = lax.dot_general(high, low_tile, dims, preferred_element_type=F32)
    return both[: v.shape[0]] + both[v.shape[0] :] + rest


def side_sums(pairs):
    n = pairs[0][0].shape[0]
    lane = lax.broadcasted_iota(I32, (n, 128), 1)
    wide = jnp.zeros((n, 128), F32)
    for i, (first, second) in enumerate(pairs):
        wide = jnp.where(lane == i, jnp.sum(first * second, axis=1, keepdims=True), wide)
    return wide


def stack_to_rows(stack):
    return jnp.transpose(jnp.concatenate(stack + [jnp.zeros((128 - C, 128), F32)], axis=0))[0:8]


def rows_to_columns(tile):
    wide = jnp.concatenate([tile, jnp.zeros((120, 128), F32)], axis=0)
    return jnp.transpose(wide)[0:C]


class Place:
    def __init__(self):
        self.row = lax.axis_index("row")
        self.col = lax.axis_index("col")
        col = self.col
        self.core = lax.rem(col, 2)
        x, y = lax.rem(col // 2, SIDE), col // (2 * SIDE)
        core = self.core
        self.a, self.b = x + core * (y - x), y + core * (x - y)
        self.sa, self.sb = 2 + 6 * core, 8 - 6 * core
        self.sibling = col + 1 - 2 * core

    def block(self, da, db):
        return (
            lax.rem(self.a + da + SIDE, SIDE) * self.sa
            + lax.rem(self.b + db + SIDE, SIDE) * self.sb
            + self.core
        )

    def sibling_block(self, da, db):
        return (
            lax.rem(self.b + da + SIDE, SIDE) * self.sb
            + lax.rem(self.a + db + SIDE, SIDE) * self.sa
            + (1 - self.core)
        )


class Gather:
    def __init__(self, place, panel, straight, send_sem, recv_sems):
        self.straight = straight
        self.p, self.panel, self.ss, self.rs = place, panel, send_sem, recv_sems

    def copy(self, part, device, index):
        return pltpu.make_async_remote_copy(
            part, part, self.ss, self.rs.at[index], device_id=(self.p.row, device), device_id_type=MESH
        )

    def send(self, slot, device, index, half=None):
        part = self.panel.at[slot] if half is None else self.panel.at[slot, pl.ds(half * HALF, HALF)]
        self.copy(part, device, index).start()

    def wait(self, index, blocks):
        self.copy(self.panel.at[pl.ds(0, blocks)], self.p.sibling, index).wait_recv()

    def along_b(self, i):
        p = self.p
        slot = p.block(OFFS[i], 0)
        self.send(slot, p.block(0, 1), 3 + i)
        self.send(slot, p.block(0, -1), 3 + i)
        if self.straight:
            self.send(slot, p.block(0, 2), 7 + i)
        self.send(slot, p.sibling, 11)

    def begin(self):
        p = self.p
        for n, da in enumerate((1, -1, 2)):
            self.send(p.col, p.block(da, 0), n)
        self.along_b(0)

    def first(self):
        for i in (1, 2, 3):
            self.wait(i - 1, 1)
            self.along_b(i)

    def second(self, i):
        p = self.p
        self.wait(3 + i, 2)
        for half, db in () if self.straight else ((0, -1), (1, 1)):
            self.send(p.block(OFFS[i], db), p.block(0, -db), 7 + i, half)
        for db in (-1, 1):
            self.send(p.block(OFFS[i], db), p.sibling, 11)

    def third(self, i):
        self.wait(7 + i, 1)
        self.send(self.p.block(OFFS[i], 2), self.p.sibling, 11)

    def end(self):
        self.wait(11, SIDE * SIDE)

    def drain(self):
        sent = 3 + 2 * SIDE + SIDE + SIDE * SIDE
        self.copy(self.panel.at[pl.ds(0, sent)], self.p.sibling, 11).wait_send()


class Scatter:
    def __init__(self, place, panel, term, other, fwd_out, fwd_in, main_out, main_in, last_out, last_in, ss, rs, own, theirs):
        self.p, self.panel, self.term, self.other = place, panel, term, other
        self.fwd_out, self.fwd_in = fwd_out, fwd_in
        self.main_out, self.main_in = main_out, main_in
        self.last_out, self.last_in = last_out, last_in
        self.ss, self.rs, self.own, self.theirs = ss, rs, own, theirs

    def copy(self, src, dst, device, index):
        return pltpu.make_async_remote_copy(
            src, dst, self.ss, self.rs.at[index], device_id=(self.p.row, device), device_id_type=MESH
        )

    def send(self, *args):
        self.copy(*args).start()

    def wait(self, ref, index):
        self.copy(ref, ref, self.p.sibling, index).wait_recv()

    def begin(self):
        every = pl.ds(0, K)
        self.send(self.term.at[every], self.other.at[every], self.p.sibling, 0)

    def share(self, da, db):
        block = self.p.block(da, db)
        return self.term[self.own[block]] + self.other[self.theirs[block]]

    def forward(self):
        self.wait(self.other.at[pl.ds(0, K)], 0)
        for side, da in ((0, 1), (1, -1)):
            for j in (0, 1):
                self.fwd_out[side, j] = self.share(2, OFFS[2 * side + j])
            self.send(self.fwd_out.at[side], self.fwd_in.at[side], self.p.block(da, 0), 1)

    def main(self, side, j, extra=None):
        da = 1 - 2 * side
        value = self.share(da, OFFS[j])
        if extra is not None:
            value = value + self.fwd_in[side, extra]
        self.main_out[j, side] = value
        self.send(self.main_out.at[j, side], self.main_in.at[j, side], self.p.block(da, 0), 2 + j)

    def main_free(self):
        for j in (0, 1):
            self.main(0, 2 + j)
            self.main(1, j)

    def main_rest(self):
        self.wait(self.fwd_in, 1)
        for j in (0, 1):
            self.main(0, j, j)
            self.main(1, 2 + j, j)

    def last(self):
        for j in (3, 1, 2, 0):
            self.wait(self.main_in.at[j], 2 + j)
            self.last_out[j] = self.share(0, OFFS[j]) + self.main_in[j, 0] + self.main_in[j, 1]
            if j:
                self.send(self.last_out.at[j], self.last_in.at[j - 1], self.p.block(0, OFFS[j]), 6)

    def result(self):
        self.wait(self.last_in, 6)
        return self.last_out[0] + self.last_in[0] + self.last_in[1] + self.last_in[2]

    def drain(self):
        sent = K + 4 + 2 * SIDE + SIDE - 1
        part = self.panel.at[pl.ds(0, sent)]
        self.copy(part, part, self.p.sibling, 6).wait_send()


class Total:
    def __init__(self, place, source, mid, plane_in, depth_in, sems):
        self.p, self.source, self.mid, self.plane_in, self.depth_in = place, source, mid, plane_in, depth_in
        self.pss, self.prs, self.dss, self.drs = sems

    def plane_copy(self, d):
        p = self.p
        device = lax.rem(p.col + d, PLANE)
        return pltpu.make_async_remote_copy(
            self.source(device), self.plane_in.at[d], self.pss, self.prs,
            device_id=(p.row, device), device_id_type=MESH,
        )

    def depth_copy(self, d):
        p = self.p
        return pltpu.make_async_remote_copy(
            self.mid, self.depth_in.at[d], self.dss, self.drs,
            device_id=(lax.rem(p.row + d, DEPTH), p.col), device_id_type=MESH,
        )

    def begin(self):
        pl.loop(1, PLANE)(lambda d: self.plane_copy(d).start())

    def whole(self, ref, count, send_sem, recv_sem):
        part = ref.at[pl.ds(1, count - 1)]
        return pltpu.make_async_remote_copy(
            part, part, send_sem, recv_sem, device_id=(self.p.row, self.p.sibling), device_id_type=MESH
        )

    def plane_whole(self):
        return self.whole(self.plane_in, PLANE, self.pss, self.prs)

    def depth_whole(self):
        return self.whole(self.depth_in, DEPTH, self.dss, self.drs)

    def middle(self, own):
        self.plane_whole().wait_recv()
        total = own
        for d in range(1, PLANE):
            total = total + self.plane_in[d]
        self.mid[...] = total
        pl.loop(1, DEPTH)(lambda d: self.depth_copy(d).start())

    def end(self):
        self.depth_whole().wait_recv()
        total = self.mid[...]
        for d in range(1, DEPTH):
            total = total + self.depth_in[d]
        return total

    def drain(self):
        self.plane_whole().wait_send()
        self.depth_whole().wait_send()


def kernel(
    diag_hbm, pairs_hbm, pattern, newton_diag_hbm, newton_pairs_hbm, warm_hbm, targets,
    out, hess,
    tiles, newton_tiles, xh, xl, nh, nl,
    gw0, gw1, gr0, gr1, gq0, gq1,
    *refs,
):
    refs = list(refs)
    n_scatter = 2 * PARTS
    buffers = [[refs.pop(0) for _ in range(8)] for _ in range(n_scatter)]
    (
        names_out, names_in, names, own_table, sibling_table,
        unit, padded, padded_image, right, right_image, message,
        tile, tile_mid, message_mid, tile_plane, tile_depth, message_plane, message_depth,
        load_sems, name_sems,
        ag_ss, ag_rs, rs_ss, rs_rs, pss, prs, dss, drs,
    ) = refs
    p = Place()
    barrier = pltpu.get_barrier_semaphore()

    @pl.loop(1, PLANE)
    def _(d):
        pl.semaphore_signal(barrier, inc=1, device_id=(p.row, lax.rem(p.col + d, PLANE)), device_id_type=MESH)

    @pl.loop(1, DEPTH)
    def _(d):
        pl.semaphore_signal(barrier, inc=1, device_id=(lax.rem(p.row + d, DEPTH), p.col), device_id_type=MESH)

    loads = [
        pltpu.make_async_copy(warm_hbm.at[0, pl.ds(0, W)], gw0.at[p.col], load_sems.at[0]),
        pltpu.make_async_copy(warm_hbm.at[0, pl.ds(W, W)], gw1.at[p.col], load_sems.at[5]),
        pltpu.make_async_copy(pairs_hbm.at[0], tiles.at[pl.ds(0, K)], load_sems.at[1]),
        pltpu.make_async_copy(diag_hbm.at[0], tiles.at[K], load_sems.at[2]),
        pltpu.make_async_copy(newton_pairs_hbm.at[0], newton_tiles.at[pl.ds(0, K)], load_sems.at[3]),
        pltpu.make_async_copy(newton_diag_hbm.at[0], newton_tiles.at[K], load_sems.at[4]),
    ]
    for load in loads:
        load.start()

    first_col = p.row * PLANE

    def fill_table(table, source):
        @pl.loop(0, PLANE)
        def _(block):
            at = jnp.int32(ZERO_TERM)
            for k in range(K):
                at = jnp.where(source[0, k] - first_col == block, k, at)
            table[block] = at

    lane = lax.broadcasted_iota(I32, (8, 128), 1)
    table = jnp.full((8, 128), -1, I32)
    for k in range(K):
        table = jnp.where(lane == k, pattern[0, k], table)
    names_out[...] = table
    panels = ((gw0, gw1), (gr0, gr1), (gq0, gq1))
    loads[0].wait()
    loads[1].wait()
    pl.semaphore_wait(barrier, PLANE + DEPTH - 2)

    def pick(k):
        inside = jnp.clip(pattern[0, k] - first_col, 0, PLANE - 1)
        return jnp.where(pattern[0, k] >= 0, inside, ZERO_BLOCK)

    gathers = [
        [Gather(p, panels[v][h], (v, h) in STRAIGHT, ag_ss.at[v * PARTS + h], ag_rs.at[v * PARTS + h]) for h in range(PARTS)]
        for v in range(3)
    ]
    scatters = [
        [
            Scatter(p, panels[v][h], *buffers[v * PARTS + h], rs_ss.at[v * PARTS + h], rs_rs.at[v * PARTS + h], own_table, sibling_table)
            for h in range(PARTS)
        ]
        for v in range(2)
    ]

    def begin(v, h):
        gathers[v][h].begin()
        if v < 2:
            scatter = scatters[v][h]
            value = panels[v][h][p.col]
            for k in range(K):
                scatter.term[k] = product(value, xh[k], xl[k], NN)
            scatter.begin()

    def first(v, h):
        if v < 2:
            scatters[v][h].forward()
            scatters[v][h].main_free()
        gathers[v][h].first()

    def second(v, h):
        if v < 2:
            scatters[v][h].main_rest()
        for i in range(SIDE):
            gathers[v][h].second(i)

    def third(v, h):
        if v < 2:
            scatters[v][h].last()
        for i in range(SIDE):
            gathers[v][h].third(i)

    def image(v, h):
        panel = panels[v][h]
        total = lax.dot_general(panel[p.col], tiles[K], NT, precision=HIGHEST, preferred_element_type=F32)
        gathers[v][h].end()
        for k in range(K):
            total = total + product(panel[pick(k)], xh[k], xl[k], NT)
        return total + scatters[v][h].result()

    def residual(h):
        panels[1][h][p.col] = unit[h * W : (h + 1) * W] - image(0, h)

    def q_image(h):
        panels[2][h][p.col] = image(1, h)

    def both_parts(f, block):
        return jnp.concatenate([f(h, block) for h in range(PARTS)], axis=0)

    def make_units():
        position = lax.broadcasted_iota(I32, (1, B), 1) + (p.row * PLANE + p.col) * B

        @pl.loop(0, C)
        def _(c):
            unit[pl.ds(c, 1), :] = (position == targets[c]).astype(F32)

    def split_newton():
        loads[4].wait()
        loads[5].wait()
        for k in range(K + 1):
            nh[k], nl[k] = split(newton_tiles[k])

    stacks = []

    def own_sums_of(h):
        r, q = panels[1][h][p.col], panels[2][h][p.col]
        stacks.append(side_sums([(r, r), (r, q), (q, q)]))

    gathers[0][0].begin()
    name_copy = pltpu.make_async_remote_copy(
        names_out, names_in, name_sems.at[0], name_sems.at[1], device_id=(p.row, p.sibling), device_id_type=MESH
    )
    name_copy.start()
    gathers[0][1].begin()
    loads[2].wait()
    value = both_parts(lambda h, block: panels[0][h][block], p.col)
    for k in range(K):
        xh[k], xl[k] = split(tiles[k])
        term = product(value, xh[k], xl[k], NN)
        for h in range(PARTS):
            scatters[0][h].term[k] = term[h * W : (h + 1) * W]
    for h in range(PARTS):
        scatters[0][h].begin()
    loads[3].wait()
    xh[K], xl[K] = split(tiles[K])
    for pair in panels:
        for g in pair:
            g[ZERO_BLOCK] = jnp.zeros((W, B), F32)
    for group in buffers:
        for t in group[:2]:
            t[ZERO_TERM] = jnp.zeros((W, B), F32)
    fill_table(own_table, pattern)
    name_copy.wait()
    name_load = pltpu.make_async_copy(names_in, names, name_sems.at[2])
    name_load.start()
    name_load.wait()
    fill_table(sibling_table, names)

    first(0, 0)
    first(0, 1)
    second(0, 0)
    make_units()
    third(0, 0)
    second(0, 1)
    residual(0)
    begin(1, 0)
    third(0, 1)
    first(1, 0)
    residual(1)
    begin(1, 1)
    second(1, 0)
    first(1, 1)
    split_newton()
    third(1, 0)
    second(1, 1)
    q_image(0)
    begin(2, 0)
    third(1, 1)
    first(2, 0)
    own_sums_of(0)
    q_image(1)
    begin(2, 1)

    sums = Total(p, lambda _: tile, tile_mid, tile_plane, tile_depth, (pss.at[0], prs.at[0], dss.at[0], drs.at[0]))
    own_sums_of(1)
    own_sums = stack_to_rows(stacks)
    tile[...] = own_sums
    sums.begin()
    second(2, 0)
    first(2, 1)
    sums.middle(own_sums)
    third(2, 0)
    second(2, 1)
    third(2, 1)
    totals = sums.end()
    norm, curve, square = totals[0:1], totals[1:2], totals[2:3]
    step = norm / curve
    norm_next = step * step * square - 2.0 * step * curve + norm
    beta = norm_next / norm
    rows = lax.broadcasted_iota(I32, (8, 128), 0)
    weights = rows_to_columns(jnp.where(rows == 0, step, beta))

    def weight(h):
        part = weights[h * W : (h + 1) * W]
        return part[:, 0:1], 1.0 + part[:, 1:2]

    def estimate(h, block):
        return gw(h)[block] + weight(h)[0] * gr(h)[block]

    def direction(h, block):
        step_c, scale = weight(h)
        return scale * gr(h)[block] - step_c * gq(h)[block]

    def gw(h):
        return panels[0][h]

    def gr(h):
        return panels[1][h]

    def gq(h):
        return panels[2][h]

    estimate_image = jnp.zeros((C, B), F32)
    for k in range(K):
        estimate_image = estimate_image + product(both_parts(estimate, pick(k)), nh[k], nl[k], NT)
    u = both_parts(estimate, p.col)
    estimate_full = estimate_image + product(u, nh[K], nl[K], NT)
    for h in range(PARTS):
        gathers[2][h].end()

    d = both_parts(direction, p.col)
    half_image = 0.5 * product(d, xh[K], xl[K], NT)
    direction_image = jnp.zeros((C, B), F32)
    for k in range(K):
        picked = both_parts(direction, pick(k))
        half_image = half_image + product(picked, xh[k], xl[k], NT)
        direction_image = direction_image + product(picked, nh[k], nl[k], NT)
    direction_full = direction_image + product(d, nh[K], nl[K], NT)
    curve_next = stack_to_rows([side_sums([(d, 2.0 * half_image)])])

    for j in range(PLANE):
        rows3 = slice(3 * j, 3 * j + 3)
        for ref, first_half, second_half in ((padded, u, d), (padded_image, estimate_image, direction_image)):
            ref[pl.ds(8 * j, 3)] = first_half[rows3]
            ref[pl.ds(8 * j + 3, 3)] = second_half[rows3]
            ref[pl.ds(8 * j + 6, 2)] = jnp.zeros((2, B), F32)
    fill = jnp.zeros((128 - C, B), F32)
    right[...] = jnp.concatenate([u, fill, d, fill], axis=0)
    right_image[...] = jnp.concatenate([estimate_full, fill, direction_full, fill], axis=0)
    pair_sums = lax.dot_general(
        padded[...], right_image[...], NT, precision=HIGHEST, preferred_element_type=F32
    ) + lax.dot_general(padded_image[...], right[...], NT, precision=HIGHEST, preferred_element_type=F32)
    curve_row = jnp.concatenate([curve_next[0:1], jnp.zeros((1, 128), F32)], axis=1)
    row_of = lax.broadcasted_iota(I32, (8, 256), 0)
    for j in range(PLANE):
        message[j] = jnp.where(row_of == 6, curve_row, pair_sums[8 * j : 8 * j + 8])
    last = Total(
        p, lambda device: message.at[device], message_mid, message_plane, message_depth,
        (pss.at[1], prs.at[1], dss.at[1], drs.at[1]),
    )
    last.begin()
    for v in range(3):
        for h in range(PARTS):
            gathers[v][h].drain()
            if v < 2:
                scatters[v][h].drain()
    sums.drain()
    last.middle(message[p.col])
    total = last.end()
    last.drain()
    step_next = norm_next / total[6:7, 0:128]
    spread = rows_to_columns(jnp.broadcast_to(step_next, (8, 128)))
    out[0] = u + spread[:, 0:1] * d
    lane8 = lax.broadcasted_iota(I32, (8, 128), 1)
    row8 = lax.broadcasted_iota(I32, (8, 128), 0)
    mine = lane8 == row8 + (C // PLANE) * p.col
    step_rows = jnp.sum(jnp.where(mine, step_next, 0.0), axis=1, keepdims=True)[0:3]
    block_rows = total[0:3, 0:128] + step_next * total[0:3, 128:256]
    block_rows = block_rows + step_rows * (total[3:6, 0:128] + step_next * total[3:6, 128:256])
    block_rows = jnp.where(lane8[0:3] < C, block_rows, 0.0)
    block_rows = jnp.concatenate([block_rows, jnp.zeros((5, 128), F32)], axis=0)
    row_index = lax.broadcasted_iota(I32, (16, 128), 0)
    lane_index = lax.broadcasted_iota(I32, (16, 128), 1)
    chooser = (lane_index == row_index + (C // DEPTH) * p.row).astype(F32)
    picked = lax.dot_general(block_rows, chooser, NT, precision=HIGHEST, preferred_element_type=F32)
    hess[...] = picked[0 : C // PLANE, 0 : C // DEPTH]


def hand_over(panel_in, hess_in, panel_out, hess_out):
    panel_out[...] = panel_in[...]
    hess_out[...] = hess_in[...]


def on_device(precision_diag, precision_pairs, pattern_cols, newton_diag, newton_pairs, warm_start, target_rows):
    block = (W, B)
    hbm = pl.BlockSpec(memory_space=pl.ANY)
    smem = pl.BlockSpec(memory_space=pltpu.SMEM)
    vmem = pl.BlockSpec(memory_space=pltpu.VMEM)
    panel = pltpu.VMEM((PLANE + 1,) + block, F32)
    terms = pltpu.VMEM((K + 1,) + block, F32)
    pair_of = pltpu.VMEM((2, 2) + block, F32)
    eight = pltpu.VMEM((SIDE, 2) + block, F32)
    four, three = pltpu.VMEM((SIDE,) + block, F32), pltpu.VMEM((SIDE - 1,) + block, F32)
    scatter = [terms, terms, pair_of, pair_of, eight, eight, four, three]
    square = pltpu.VMEM((8 * PLANE, B), F32)
    tile, message = (8, 128), (8, 256)
    dma = pltpu.SemaphoreType.DMA
    panel_out, hessian = pl.pallas_call(
        kernel,
        out_shape=(jax.ShapeDtypeStruct((1, C, B), F32), jax.ShapeDtypeStruct((C // PLANE, C // DEPTH), F32)),
        in_specs=[hbm, hbm, smem, hbm, hbm, hbm, smem],
        out_specs=(vmem, vmem),
        scratch_shapes=[
            pltpu.VMEM((K + 1, B, B), F32), pltpu.VMEM((K + 1, B, B), F32),
            pltpu.VMEM((K + 1, B, B), BF16), pltpu.VMEM((K + 1, B, B), BF16),
            pltpu.VMEM((K + 1, B, B), BF16), pltpu.VMEM((K + 1, B, B), BF16),
            *[panel] * (3 * PARTS),
            *scatter * (2 * PARTS),
            pltpu.VMEM((8, 128), I32), pltpu.VMEM((8, 128), I32), pltpu.SMEM((8, 128), I32),
            pltpu.SMEM((PLANE,), I32), pltpu.SMEM((PLANE,), I32),
            pltpu.VMEM((C, B), F32), square, square, square, square,
            pltpu.VMEM((PLANE,) + message, F32),
            pltpu.VMEM(tile, F32), pltpu.VMEM(tile, F32), pltpu.VMEM(message, F32),
            pltpu.VMEM((PLANE,) + tile, F32), pltpu.VMEM((DEPTH,) + tile, F32),
            pltpu.VMEM((PLANE,) + message, F32), pltpu.VMEM((DEPTH,) + message, F32),
            dma((6,)), dma((3,)),
            dma((3 * PARTS,)), dma((3 * PARTS, N_AG)), dma((2 * PARTS,)), dma((2 * PARTS, N_RS)),
            dma((2,)), dma((2,)), dma((2,)), dma((2,)),
        ],
        compiler_params=pltpu.CompilerParams(
            collective_id=0, has_side_effects=True, vmem_limit_bytes=58 * 2**20
        ),
    )(precision_diag, precision_pairs, pattern_cols, newton_diag, newton_pairs, warm_start, target_rows)
    panel_out, hessian = pl.pallas_call(
        hand_over,
        out_shape=(jax.ShapeDtypeStruct((1, C, B), F32), jax.ShapeDtypeStruct((C // PLANE, C // DEPTH), F32)),
        in_specs=[vmem, vmem],
        out_specs=(vmem, vmem),
    )(panel_out, hessian)
    return panel_out, hessian.T


def solution(mesh):
    both = ("row", "col")
    placed = (
        P(both, None, None),
        P(both, None, None, None),
        P(both, None),
        P(both, None, None),
        P(both, None, None, None),
        P(both, None, None),
        P(),
    )
    return jax.shard_map(
        on_device,
        mesh=mesh,
        in_specs=placed,
        out_specs=(P(both, None, None), P("row", "col")),
        check_vma=False,
    )
```

```python
import jax
import jax.numpy as jnp
from jax import lax
from jax.experimental import pallas as pl
from jax.experimental.pallas import tpu as pltpu
from jax.sharding import PartitionSpec as P

HIGHEST = lax.Precision.HIGHEST
MESH = pl.DeviceIdType.MESH
F32, BF16, I32 = jnp.float32, jnp.bfloat16, jnp.int32
C, B, K = 96, 256, 7
PARTS = 2
W = C // PARTS
HALF = W // 2
PLANE, DEPTH, SIDE = 32, 8, 4
NT = (((1,), (1,)), ((), ()))
NN = (((1,), (0,)), ((), ()))
OFFS = (0, -1, 1, 2)
ZERO_BLOCK = PLANE
ZERO_TERM = K
N_AG, N_RS = 12, 7
STRAIGHT = ((2, 1),)


def split(v):
    high = v.astype(BF16)
    return high, (v - high.astype(F32)).astype(BF16)


def product(v, high_tile, low_tile, dims):
    high, low = split(v)
    both = lax.dot_general(
        jnp.concatenate([high, low], axis=0), high_tile, dims, preferred_element_type=F32
    )
    rest = lax.dot_general(high, low_tile, dims, preferred_element_type=F32)
    return both[: v.shape[0]] + both[v.shape[0] :] + rest


def side_sums(pairs):
    n = pairs[0][0].shape[0]
    lane = lax.broadcasted_iota(I32, (n, 128), 1)
    wide = jnp.zeros((n, 128), F32)
    for i, (first, second) in enumerate(pairs):
        wide = jnp.where(lane == i, jnp.sum(first * second, axis=1, keepdims=True), wide)
    return wide


def stack_to_rows(stack):
    return jnp.transpose(jnp.concatenate(stack + [jnp.zeros((128 - C, 128), F32)], axis=0))[0:8]


def rows_to_columns(tile):
    wide = jnp.concatenate([tile, jnp.zeros((120, 128), F32)], axis=0)
    return jnp.transpose(wide)[0:C]


class Place:
    def __init__(self):
        self.row = lax.axis_index("row")
        self.col = lax.axis_index("col")
        col = self.col
        self.core = lax.rem(col, 2)
        x, y = lax.rem(col // 2, SIDE), col // (2 * SIDE)
        core = self.core
        self.a, self.b = x + core * (y - x), y + core * (x - y)
        self.sa, self.sb = 2 + 6 * core, 8 - 6 * core
        self.sibling = col + 1 - 2 * core

    def block(self, da, db):
        return (
            lax.rem(self.a + da + SIDE, SIDE) * self.sa
            + lax.rem(self.b + db + SIDE, SIDE) * self.sb
            + self.core
        )

    def sibling_block(self, da, db):
        return (
            lax.rem(self.b + da + SIDE, SIDE) * self.sb
            + lax.rem(self.a + db + SIDE, SIDE) * self.sa
            + (1 - self.core)
        )


class Gather:
    def __init__(self, place, panel, straight, send_sem, recv_sems):
        self.straight = straight
        self.p, self.panel, self.ss, self.rs = place, panel, send_sem, recv_sems

    def copy(self, part, device, index):
        return pltpu.make_async_remote_copy(
            part, part, self.ss, self.rs.at[index], device_id=(self.p.row, device), device_id_type=MESH
        )

    def send(self, slot, device, index, half=None):
        part = self.panel.at[slot] if half is None else self.panel.at[slot, pl.ds(half * HALF, HALF)]
        self.copy(part, device, index).start()

    def wait(self, index, blocks):
        self.copy(self.panel.at[pl.ds(0, blocks)], self.p.sibling, index).wait_recv()

    def along_b(self, i):
        p = self.p
        slot = p.block(OFFS[i], 0)
        self.send(slot, p.block(0, 1), 3 + i)
        self.send(slot, p.block(0, -1), 3 + i)
        if self.straight:
            self.send(slot, p.block(0, 2), 7 + i)
        self.send(slot, p.sibling, 11)

    def begin(self):
        p = self.p
        for n, da in enumerate((1, -1, 2)):
            self.send(p.col, p.block(da, 0), n)
        self.along_b(0)

    def first(self):
        for i in (1, 2, 3):
            self.wait(i - 1, 1)
            self.along_b(i)

    def second(self, i):
        p = self.p
        self.wait(3 + i, 2)
        for half, db in () if self.straight else ((0, -1), (1, 1)):
            self.send(p.block(OFFS[i], db), p.block(0, -db), 7 + i, half)
        for db in (-1, 1):
            self.send(p.block(OFFS[i], db), p.sibling, 11)

    def third(self, i):
        self.wait(7 + i, 1)
        self.send(self.p.block(OFFS[i], 2), self.p.sibling, 11)

    def end(self):
        self.wait(11, SIDE * SIDE)

    def drain(self):
        sent = 3 + 2 * SIDE + SIDE + SIDE * SIDE
        self.copy(self.panel.at[pl.ds(0, sent)], self.p.sibling, 11).wait_send()


class Scatter:
    def __init__(self, place, panel, term, other, fwd_out, fwd_in, main_out, main_in, last_out, last_in, ss, rs, own, theirs):
        self.p, self.panel, self.term, self.other = place, panel, term, other
        self.fwd_out, self.fwd_in = fwd_out, fwd_in
        self.main_out, self.main_in = main_out, main_in
        self.last_out, self.last_in = last_out, last_in
        self.ss, self.rs, self.own, self.theirs = ss, rs, own, theirs

    def copy(self, src, dst, device, index):
        return pltpu.make_async_remote_copy(
            src, dst, self.ss, self.rs.at[index], device_id=(self.p.row, device), device_id_type=MESH
        )

    def send(self, *args):
        self.copy(*args).start()

    def wait(self, ref, index):
        self.copy(ref, ref, self.p.sibling, index).wait_recv()

    def begin(self):
        every = pl.ds(0, K)
        self.send(self.term.at[every], self.other.at[every], self.p.sibling, 0)

    def share(self, da, db):
        block = self.p.block(da, db)
        return self.term[self.own[block]] + self.other[self.theirs[block]]

    def forward(self):
        self.wait(self.other.at[pl.ds(0, K)], 0)
        for side, da in ((0, 1), (1, -1)):
            for j in (0, 1):
                self.fwd_out[side, j] = self.share(2, OFFS[2 * side + j])
            self.send(self.fwd_out.at[side], self.fwd_in.at[side], self.p.block(da, 0), 1)

    def main(self, side, j, extra=None):
        da = 1 - 2 * side
        value = self.share(da, OFFS[j])
        if extra is not None:
            value = value + self.fwd_in[side, extra]
        self.main_out[j, side] = value
        self.send(self.main_out.at[j, side], self.main_in.at[j, side], self.p.block(da, 0), 2 + j)

    def main_free(self):
        for j in (0, 1):
            self.main(0, 2 + j)
            self.main(1, j)

    def main_rest(self):
        self.wait(self.fwd_in, 1)
        for j in (0, 1):
            self.main(0, j, j)
            self.main(1, 2 + j, j)

    def last(self):
        for j in (3, 1, 2, 0):
            self.wait(self.main_in.at[j], 2 + j)
            self.last_out[j] = self.share(0, OFFS[j]) + self.main_in[j, 0] + self.main_in[j, 1]
            if j:
                self.send(self.last_out.at[j], self.last_in.at[j - 1], self.p.block(0, OFFS[j]), 6)

    def result(self):
        self.wait(self.last_in, 6)
        return self.last_out[0] + self.last_in[0] + self.last_in[1] + self.last_in[2]

    def drain(self):
        sent = K + 4 + 2 * SIDE + SIDE - 1
        part = self.panel.at[pl.ds(0, sent)]
        self.copy(part, part, self.p.sibling, 6).wait_send()


class Total:
    def __init__(self, place, source, mid, plane_in, depth_in, sems):
        self.p, self.source, self.mid, self.plane_in, self.depth_in = place, source, mid, plane_in, depth_in
        self.pss, self.prs, self.dss, self.drs = sems

    def plane_copy(self, d):
        p = self.p
        device = lax.rem(p.col + d, PLANE)
        return pltpu.make_async_remote_copy(
            self.source(device), self.plane_in.at[d], self.pss, self.prs,
            device_id=(p.row, device), device_id_type=MESH,
        )

    def depth_copy(self, d):
        p = self.p
        return pltpu.make_async_remote_copy(
            self.mid, self.depth_in.at[d], self.dss, self.drs,
            device_id=(lax.rem(p.row + d, DEPTH), p.col), device_id_type=MESH,
        )

    def begin(self):
        pl.loop(1, PLANE)(lambda d: self.plane_copy(d).start())

    def whole(self, ref, count, send_sem, recv_sem):
        part = ref.at[pl.ds(1, count - 1)]
        return pltpu.make_async_remote_copy(
            part, part, send_sem, recv_sem, device_id=(self.p.row, self.p.sibling), device_id_type=MESH
        )

    def plane_whole(self):
        return self.whole(self.plane_in, PLANE, self.pss, self.prs)

    def depth_whole(self):
        return self.whole(self.depth_in, DEPTH, self.dss, self.drs)

    def middle(self, own):
        self.plane_whole().wait_recv()
        total = own
        for d in range(1, PLANE):
            total = total + self.plane_in[d]
        self.mid[...] = total
        pl.loop(1, DEPTH)(lambda d: self.depth_copy(d).start())

    def end(self):
        self.depth_whole().wait_recv()
        total = self.mid[...]
        for d in range(1, DEPTH):
            total = total + self.depth_in[d]
        return total

    def drain(self):
        self.plane_whole().wait_send()
        self.depth_whole().wait_send()


def kernel(
    diag_hbm, pairs_hbm, pattern, newton_diag_hbm, newton_pairs_hbm, warm_hbm, targets,
    out, hess,
    tiles, newton_tiles, xh, xl, nh, nl,
    gw0, gw1, gr0, gr1, gq0, gq1,
    *refs,
):
    refs = list(refs)
    n_scatter = 2 * PARTS
    buffers = [[refs.pop(0) for _ in range(8)] for _ in range(n_scatter)]
    (
        names_out, names_in, names, own_table, sibling_table,
        unit, padded, padded_image, right, right_image, message,
        tile, tile_mid, message_mid, tile_plane, tile_depth, message_plane, message_depth,
        load_sems, name_sems,
        ag_ss, ag_rs, rs_ss, rs_rs, pss, prs, dss, drs,
    ) = refs
    p = Place()
    barrier = pltpu.get_barrier_semaphore()

    @pl.loop(1, PLANE)
    def _(d):
        pl.semaphore_signal(barrier, inc=1, device_id=(p.row, lax.rem(p.col + d, PLANE)), device_id_type=MESH)

    @pl.loop(1, DEPTH)
    def _(d):
        pl.semaphore_signal(barrier, inc=1, device_id=(lax.rem(p.row + d, DEPTH), p.col), device_id_type=MESH)

    loads = [
        pltpu.make_async_copy(warm_hbm.at[0, pl.ds(0, W)], gw0.at[p.col], load_sems.at[0]),
        pltpu.make_async_copy(warm_hbm.at[0, pl.ds(W, W)], gw1.at[p.col], load_sems.at[5]),
        pltpu.make_async_copy(pairs_hbm.at[0], tiles.at[pl.ds(0, K)], load_sems.at[1]),
        pltpu.make_async_copy(diag_hbm.at[0], tiles.at[K], load_sems.at[2]),
        pltpu.make_async_copy(newton_pairs_hbm.at[0], newton_tiles.at[pl.ds(0, K)], load_sems.at[3]),
        pltpu.make_async_copy(newton_diag_hbm.at[0], newton_tiles.at[K], load_sems.at[4]),
    ]
    for load in loads:
        load.start()

    first_col = p.row * PLANE

    def fill_table(table, source):
        @pl.loop(0, PLANE)
        def _(block):
            at = jnp.int32(ZERO_TERM)
            for k in range(K):
                at = jnp.where(source[0, k] - first_col == block, k, at)
            table[block] = at

    lane = lax.broadcasted_iota(I32, (8, 128), 1)
    table = jnp.full((8, 128), -1, I32)
    for k in range(K):
        table = jnp.where(lane == k, pattern[0, k], table)
    names_out[...] = table
    panels = ((gw0, gw1), (gr0, gr1), (gq0, gq1))
    loads[0].wait()
    loads[1].wait()
    pl.semaphore_wait(barrier, PLANE + DEPTH - 2)

    def pick(k):
        inside = jnp.clip(pattern[0, k] - first_col, 0, PLANE - 1)
        return jnp.where(pattern[0, k] >= 0, inside, ZERO_BLOCK)

    gathers = [
        [Gather(p, panels[v][h], (v, h) in STRAIGHT, ag_ss.at[v * PARTS + h], ag_rs.at[v * PARTS + h]) for h in range(PARTS)]
        for v in range(3)
    ]
    scatters = [
        [
            Scatter(p, panels[v][h], *buffers[v * PARTS + h], rs_ss.at[v * PARTS + h], rs_rs.at[v * PARTS + h], own_table, sibling_table)
            for h in range(PARTS)
        ]
        for v in range(2)
    ]

    def begin(v, h):
        gathers[v][h].begin()
        if v < 2:
            scatter = scatters[v][h]
            value = panels[v][h][p.col]
            for k in range(K):
                scatter.term[k] = product(value, xh[k], xl[k], NN)
            scatter.begin()

    def first(v, h):
        if v < 2:
            scatters[v][h].forward()
            scatters[v][h].main_free()
        gathers[v][h].first()

    def second(v, h):
        if v < 2:
            scatters[v][h].main_rest()
        for i in range(SIDE):
            gathers[v][h].second(i)

    def third(v, h):
        if v < 2:
            scatters[v][h].last()
        for i in range(SIDE):
            gathers[v][h].third(i)

    def image(v, h):
        panel = panels[v][h]
        total = lax.dot_general(panel[p.col], tiles[K], NT, precision=HIGHEST, preferred_element_type=F32)
        gathers[v][h].end()
        for k in range(K):
            total = total + product(panel[pick(k)], xh[k], xl[k], NT)
        return total + scatters[v][h].result()

    def residual(h):
        panels[1][h][p.col] = unit[h * W : (h + 1) * W] - image(0, h)

    def q_image(h):
        panels[2][h][p.col] = image(1, h)

    def both_parts(f, block):
        return jnp.concatenate([f(h, block) for h in range(PARTS)], axis=0)

    def make_units():
        position = lax.broadcasted_iota(I32, (1, B), 1) + (p.row * PLANE + p.col) * B

        @pl.loop(0, C)
        def _(c):
            unit[pl.ds(c, 1), :] = (position == targets[c]).astype(F32)

    def split_newton():
        loads[4].wait()
        loads[5].wait()
        for k in range(K + 1):
            nh[k], nl[k] = split(newton_tiles[k])

    stacks = []

    def own_sums_of(h):
        r, q = panels[1][h][p.col], panels[2][h][p.col]
        stacks.append(side_sums([(r, r), (r, q), (q, q)]))

    gathers[0][0].begin()
    name_copy = pltpu.make_async_remote_copy(
        names_out, names_in, name_sems.at[0], name_sems.at[1], device_id=(p.row, p.sibling), device_id_type=MESH
    )
    name_copy.start()
    gathers[0][1].begin()
    loads[2].wait()
    value = both_parts(lambda h, block: panels[0][h][block], p.col)
    for k in range(K):
        xh[k], xl[k] = split(tiles[k])
        term = product(value, xh[k], xl[k], NN)
        for h in range(PARTS):
            scatters[0][h].term[k] = term[h * W : (h + 1) * W]
    for h in range(PARTS):
        scatters[0][h].begin()
    loads[3].wait()
    xh[K], xl[K] = split(tiles[K])
    for pair in panels:
        for g in pair:
            g[ZERO_BLOCK] = jnp.zeros((W, B), F32)
    for group in buffers:
        for t in group[:2]:
            t[ZERO_TERM] = jnp.zeros((W, B), F32)
    fill_table(own_table, pattern)
    name_copy.wait()
    name_load = pltpu.make_async_copy(names_in, names, name_sems.at[2])
    name_load.start()
    name_load.wait()
    fill_table(sibling_table, names)

    first(0, 0)
    first(0, 1)
    second(0, 0)
    make_units()
    third(0, 0)
    second(0, 1)
    residual(0)
    begin(1, 0)
    third(0, 1)
    first(1, 0)
    residual(1)
    begin(1, 1)
    second(1, 0)
    first(1, 1)
    split_newton()
    third(1, 0)
    second(1, 1)
    q_image(0)
    begin(2, 0)
    third(1, 1)
    first(2, 0)
    own_sums_of(0)
    q_image(1)
    begin(2, 1)

    sums = Total(p, lambda _: tile, tile_mid, tile_plane, tile_depth, (pss.at[0], prs.at[0], dss.at[0], drs.at[0]))
    own_sums_of(1)
    own_sums = stack_to_rows(stacks)
    tile[...] = own_sums
    sums.begin()
    second(2, 0)
    first(2, 1)
    sums.middle(own_sums)
    third(2, 0)
    second(2, 1)
    third(2, 1)
    totals = sums.end()
    norm, curve, square = totals[0:1], totals[1:2], totals[2:3]
    step = norm / curve
    norm_next = step * step * square - 2.0 * step * curve + norm
    beta = norm_next / norm
    rows = lax.broadcasted_iota(I32, (8, 128), 0)
    weights = rows_to_columns(jnp.where(rows == 0, step, beta))

    def weight(h):
        part = weights[h * W : (h + 1) * W]
        return part[:, 0:1], 1.0 + part[:, 1:2]

    def estimate(h, block):
        return gw(h)[block] + weight(h)[0] * gr(h)[block]

    def direction(h, block):
        step_c, scale = weight(h)
        return scale * gr(h)[block] - step_c * gq(h)[block]

    def gw(h):
        return panels[0][h]

    def gr(h):
        return panels[1][h]

    def gq(h):
        return panels[2][h]

    estimate_image = jnp.zeros((C, B), F32)
    for k in range(K):
        estimate_image = estimate_image + product(both_parts(estimate, pick(k)), nh[k], nl[k], NT)
    u = both_parts(estimate, p.col)
    estimate_full = estimate_image + product(u, nh[K], nl[K], NT)
    def place_rows(at, values, images):
        for j in range(PLANE):
            padded[pl.ds(8 * j + at, 3)] = values[3 * j : 3 * j + 3]
            padded_image[pl.ds(8 * j + at, 3)] = images[3 * j : 3 * j + 3]

    for ref in (padded, padded_image):
        ref[...] = jnp.zeros((8 * PLANE, B), F32)
    fill = jnp.zeros((128 - C, B), F32)
    for ref in (right, right_image):
        ref[pl.ds(C, 128 - C)] = fill
        ref[pl.ds(128 + C, 128 - C)] = fill
    place_rows(0, u, estimate_image)
    right[pl.ds(0, C)] = u
    right_image[pl.ds(0, C)] = estimate_full
    for h in range(PARTS):
        gathers[2][h].end()

    d = both_parts(direction, p.col)
    half_image = 0.5 * product(d, xh[K], xl[K], NT)
    direction_image = jnp.zeros((C, B), F32)
    for k in range(K):
        picked = both_parts(direction, pick(k))
        half_image = half_image + product(picked, xh[k], xl[k], NT)
        direction_image = direction_image + product(picked, nh[k], nl[k], NT)
    direction_full = direction_image + product(d, nh[K], nl[K], NT)
    curve_next = stack_to_rows([side_sums([(d, 2.0 * half_image)])])

    place_rows(3, d, direction_image)
    right[pl.ds(128, C)] = d
    right_image[pl.ds(128, C)] = direction_full
    pair_sums = product(padded[...], *split(right_image[...]), NT) + product(padded_image[...], *split(right[...]), NT)
    curve_row = jnp.concatenate([curve_next[0:1], jnp.zeros((1, 128), F32)], axis=1)
    row_of = lax.broadcasted_iota(I32, (8, 256), 0)
    for j in range(PLANE):
        message[j] = jnp.where(row_of == 6, curve_row, pair_sums[8 * j : 8 * j + 8])
    last = Total(
        p, lambda device: message.at[device], message_mid, message_plane, message_depth,
        (pss.at[1], prs.at[1], dss.at[1], drs.at[1]),
    )
    last.begin()
    for v in range(3):
        for h in range(PARTS):
            gathers[v][h].drain()
            if v < 2:
                scatters[v][h].drain()
    sums.drain()
    last.middle(message[p.col])
    total = last.end()
    last.drain()
    step_next = norm_next / total[6:7, 0:128]
    spread = rows_to_columns(jnp.broadcast_to(step_next, (8, 128)))
    out[0] = u + spread[:, 0:1] * d
    lane8 = lax.broadcasted_iota(I32, (8, 128), 1)
    row8 = lax.broadcasted_iota(I32, (8, 128), 0)
    mine = lane8 == row8 + (C // PLANE) * p.col
    step_rows = jnp.sum(jnp.where(mine, step_next, 0.0), axis=1, keepdims=True)[0:3]
    block_rows = total[0:3, 0:128] + step_next * total[0:3, 128:256]
    block_rows = block_rows + step_rows * (total[3:6, 0:128] + step_next * total[3:6, 128:256])
    block_rows = jnp.where(lane8[0:3] < C, block_rows, 0.0)
    block_rows = jnp.concatenate([block_rows, jnp.zeros((5, 128), F32)], axis=0)
    row_index = lax.broadcasted_iota(I32, (16, 128), 0)
    lane_index = lax.broadcasted_iota(I32, (16, 128), 1)
    chooser = (lane_index == row_index + (C // DEPTH) * p.row).astype(F32)
    picked = lax.dot_general(block_rows, chooser, NT, precision=HIGHEST, preferred_element_type=F32)
    hess[...] = picked[0 : C // PLANE, 0 : C // DEPTH]


def hand_over(panel_in, hess_in, panel_out, hess_out):
    panel_out[...] = panel_in[...]
    hess_out[...] = hess_in[...]


def on_device(precision_diag, precision_pairs, pattern_cols, newton_diag, newton_pairs, warm_start, target_rows):
    block = (W, B)
    hbm = pl.BlockSpec(memory_space=pl.ANY)
    smem = pl.BlockSpec(memory_space=pltpu.SMEM)
    vmem = pl.BlockSpec(memory_space=pltpu.VMEM)
    panel = pltpu.VMEM((PLANE + 1,) + block, F32)
    terms = pltpu.VMEM((K + 1,) + block, F32)
    pair_of = pltpu.VMEM((2, 2) + block, F32)
    eight = pltpu.VMEM((SIDE, 2) + block, F32)
    four, three = pltpu.VMEM((SIDE,) + block, F32), pltpu.VMEM((SIDE - 1,) + block, F32)
    scatter = [terms, terms, pair_of, pair_of, eight, eight, four, three]
    square = pltpu.VMEM((8 * PLANE, B), F32)
    tile, message = (8, 128), (8, 256)
    dma = pltpu.SemaphoreType.DMA
    panel_out, hessian = pl.pallas_call(
        kernel,
        out_shape=(jax.ShapeDtypeStruct((1, C, B), F32), jax.ShapeDtypeStruct((C // PLANE, C // DEPTH), F32)),
        in_specs=[hbm, hbm, smem, hbm, hbm, hbm, smem],
        out_specs=(vmem, vmem),
        scratch_shapes=[
            pltpu.VMEM((K + 1, B, B), F32), pltpu.VMEM((K + 1, B, B), F32),
            pltpu.VMEM((K + 1, B, B), BF16), pltpu.VMEM((K + 1, B, B), BF16),
            pltpu.VMEM((K + 1, B, B), BF16), pltpu.VMEM((K + 1, B, B), BF16),
            *[panel] * (3 * PARTS),
            *scatter * (2 * PARTS),
            pltpu.VMEM((8, 128), I32), pltpu.VMEM((8, 128), I32), pltpu.SMEM((8, 128), I32),
            pltpu.SMEM((PLANE,), I32), pltpu.SMEM((PLANE,), I32),
            pltpu.VMEM((C, B), F32), square, square, square, square,
            pltpu.VMEM((PLANE,) + message, F32),
            pltpu.VMEM(tile, F32), pltpu.VMEM(tile, F32), pltpu.VMEM(message, F32),
            pltpu.VMEM((PLANE,) + tile, F32), pltpu.VMEM((DEPTH,) + tile, F32),
            pltpu.VMEM((PLANE,) + message, F32), pltpu.VMEM((DEPTH,) + message, F32),
            dma((6,)), dma((3,)),
            dma((3 * PARTS,)), dma((3 * PARTS, N_AG)), dma((2 * PARTS,)), dma((2 * PARTS, N_RS)),
            dma((2,)), dma((2,)), dma((2,)), dma((2,)),
        ],
        compiler_params=pltpu.CompilerParams(
            collective_id=0, has_side_effects=True, vmem_limit_bytes=58 * 2**20
        ),
    )(precision_diag, precision_pairs, pattern_cols, newton_diag, newton_pairs, warm_start, target_rows)
    panel_out, hessian = pl.pallas_call(
        hand_over,
        out_shape=(jax.ShapeDtypeStruct((1, C, B), F32), jax.ShapeDtypeStruct((C // PLANE, C // DEPTH), F32)),
        in_specs=[vmem, vmem],
        out_specs=(vmem, vmem),
    )(panel_out, hessian)
    return panel_out, hessian.T


def solution(mesh):
    both = ("row", "col")
    placed = (
        P(both, None, None),
        P(both, None, None, None),
        P(both, None),
        P(both, None, None),
        P(both, None, None, None),
        P(both, None, None),
        P(),
    )
    return jax.shard_map(
        on_device,
        mesh=mesh,
        in_specs=placed,
        out_specs=(P(both, None, None), P("row", "col")),
        check_vma=False,
    )
```
